32 devices in a mesh: seq: 8 (over y, x, core), tensor: 4 (over z).
Axes of the slice: x: 2, y: 2, z: 4, core: 2. Of those that a mesh axis runs over, the one named last changes fastest.
Arguments:
- tokens: bfloat16 [2048, 1024], P('seq'), may hold values from -12 to 12
- cache_keys: bfloat16 [2048, 1024], P('seq', 'tensor'), may hold values from -700 to 700
- cache_values: bfloat16 [2048, 1024], P('seq', 'tensor'), may hold values from -6 to 6
- joined_weight: float32 [1024, 3072], P(('seq', 'tensor')), may hold values from -0.1875 to 0.1875
- output_weight: float32 [1024, 1024], P(('seq', 'tensor')), may hold values from -0.1875 to 0.1875
- upward_weight: float32 [1024, 4096], P(('seq', 'tensor')), may hold values from -0.1875 to 0.1875
- downward_weight: float32 [1024, 4096], P(('seq', 'tensor')), may hold values from -0.09375 to 0.09375
- first_gain: float32 [1024], replicated, may hold values from 0.1 to 1.9
- second_gain: float32 [1024], replicated, may hold values from 0.1 to 1.9
- bias_table: float32 [32, 16], P(None, 'tensor'), may hold values from -4 to 4
- bucket_index: int32 [1023], replicated, may hold values from 0 to 31, as said below
- cached_lengths: int32 [8], replicated, may hold values from 0 to 256, as said below
- new_counts: int32 [8], replicated, may hold values from 1 to 256, as said below
- extend_flags: int32 [8], replicated, may hold values 0 or 1
Outputs:
- layer_out: bfloat16 [2048, 1024], P(('seq', 'tensor'))
The draws below stay inside these ranges and needn't reach their ends.
Inputs may be any that keep to these rules, and one draw needn't show every extreme that they name: `cached_lengths`: some request has exactly 256 cached tokens. `new_counts`: slots of a request past its count are padding; some request fills all 256. `bucket_index`: entry 511 + o is the bucket of offset o; offsets o <= 0 take buckets below 16, offsets o > 0 the others, and on each side the bucket never falls as the distance grows.
All inputs are finite; a program needn't handle non-finite values.
Results may differ from the reference program's by a relative error of at most 0.015.
Values may be sent and summed in bfloat16 or wider, within the bound.
No kernel may reach another device: no remote copies, remote signals or barrier semaphores. Data moves between devices by JAX's collectives and lax.ppermute only.
A program may use at most 128 MiB of HBM per device.

```python
import jax
import jax.numpy as jnp
from jax import lax

D = 1024
HEADS = 16
HEAD = 64
FF = 4096
BUCKETS = 32
NEW = 256
CACHE_MAX = 256
SPAN = 512
REQS = 8
DA = 1024


def draw_tokens(key, part):
    first_key, second_key, third_key = jax.random.split(key, 3)
    row_scale = jnp.exp(jax.random.uniform(second_key, (REQS * NEW, 1), jnp.float32, jnp.log(0.1), 0.0))
    column_scale = jnp.exp(jax.random.uniform(third_key, (1, D), jnp.float32, jnp.log(0.1), 0.0))
    drawn = jax.random.truncated_normal(first_key, -6.0, 6.0, (REQS * NEW, D), jnp.float32)
    return (2.0 * drawn * row_scale * column_scale).astype(jnp.bfloat16)


def draw_cache_keys(key, part):
    first_key = jax.random.fold_in(key, 0)
    total_rows = REQS * CACHE_MAX
    drawn = jax.random.truncated_normal(first_key, -6.0, 6.0, (total_rows, DA), jnp.float32)
    return drawn.astype(jnp.bfloat16)


def draw_bucket_index(key, part):
    half_count = BUCKETS // 2
    exact_count = half_count // 2
    bases = exact_count * 2 ** jnp.arange(half_count - exact_count, dtype=jnp.int32)
    jitter = jax.random.randint(key, (half_count - exact_count,), 0, bases)
    limits = jnp.concatenate([jnp.arange(1, exact_count, dtype=jnp.int32), bases + jitter])
    offsets = jnp.arange(2 * SPAN - 1, dtype=jnp.int32) - (SPAN - 1)
    distance = jnp.abs(offsets)
    passed = jnp.sum((distance[:, None] >= limits[None, :]).astype(jnp.int32), axis=1)
    return (passed + half_count * (offsets > 0).astype(jnp.int32)).astype(jnp.int32)


def draw_cached_lengths(key, part):
    first_key, second_key, third_key = jax.random.split(key, 3)
    first_draw = jax.random.randint(first_key, (REQS,), 0, CACHE_MAX + 1)
    second_draw = jax.random.randint(second_key, (REQS,), 0, CACHE_MAX + 1)
    lengths = first_draw * second_draw // CACHE_MAX
    chosen = jax.random.randint(third_key, (), 0, REQS)
    return jnp.where(jnp.arange(REQS, dtype=jnp.int32) == chosen, CACHE_MAX, lengths).astype(jnp.int32)


def draw_new_counts(key, part):
    first_key, second_key = jax.random.split(key)
    counts = jax.random.randint(first_key, (REQS,), 1, NEW + 1)
    chosen = jax.random.randint(second_key, (), 0, REQS)
    return jnp.where(jnp.arange(REQS, dtype=jnp.int32) == chosen, NEW, counts).astype(jnp.int32)


def plant(values, key, low, largest):
    shape = values.shape
    place = [jax.random.randint(jax.random.fold_in(key, axis), (), 0, shape[axis]) for axis in range(len(shape))]
    values = values.at[tuple(place)].set(low)
    longest = shape.index(max(shape))
    place[longest] = (place[longest] + 1) % shape[longest]
    return values.at[tuple(place)].set(largest)


def level_of(stream_key, dims, cuts, low, high):
    def one(dim, shards_of):
        heights = jax.random.uniform(jax.random.fold_in(jax.random.fold_in(stream_key, 6), dim), (shards_of,), jnp.float32, low / len(cuts), high / len(cuts))
        return jnp.repeat(jnp.exp(heights), dims[dim] // shards_of).reshape((-1,) + (1,) * (len(dims) - dim - 1))

    loudness = one(*cuts[0])
    for cut in cuts[1:]:
        loudness = loudness * one(*cut)
    return loudness


def noise(rng, dims, width, reach, cuts=(), kind=jnp.bfloat16):
    array = jax.random.normal(rng, dims, jnp.float32) * width
    if len(cuts) > 0:
        array = level_of(rng, dims, cuts, -0.22, 0.18) * array
    return jnp.clip(array, min=-reach, max=reach).astype(kind)


def setup_inputs(seed: int = 0) -> dict:
    streams_of = jax.random.split(jax.random.key(seed), 15)
    tokens = draw_tokens(jax.random.fold_in(streams_of[14], 71), 0)
    cache_keys = draw_cache_keys(jax.random.fold_in(streams_of[14], 71), 0)
    cache_values = noise(streams_of[2], (REQS * CACHE_MAX, DA), 1.0, 6.0, ((0, 8), (1, 4)))
    joined_weight = noise(streams_of[3], (D, 3 * DA), D ** -0.5, 0.1875, ((0, 32),), jnp.float32)
    output_weight = noise(streams_of[4], (D, DA), DA ** -0.5, 0.1875, ((0, 32),), jnp.float32)
    upward_weight = noise(streams_of[5], (D, FF), D ** -0.5, 0.1875, ((0, 32),), jnp.float32)
    downward_weight = noise(streams_of[6], (D, FF), FF ** -0.5, 0.09375, ((0, 32),), jnp.float32)
    first_gain = jnp.clip(1.0 + 0.18 * jax.random.normal(streams_of[7], (D,), jnp.float32), 0.1, 1.9)
    second_gain = jnp.clip(1.0 + 0.18 * jax.random.normal(streams_of[8], (D,), jnp.float32), 0.1, 1.9)
    bias_table = noise(streams_of[9], (BUCKETS, HEADS), 1.0, 4.0, ((1, 4),), jnp.float32)
    bucket_index = draw_bucket_index(jax.random.fold_in(streams_of[14], 71), 0)
    cached_lengths = draw_cached_lengths(jax.random.fold_in(streams_of[14], 71), 0)
    new_counts = draw_new_counts(jax.random.fold_in(streams_of[14], 71), 0)
    extend_flags = plant((jax.random.randint(streams_of[13], (REQS,), 0, 4) < 3).astype(jnp.int32), jax.random.fold_in(streams_of[13], 1), 0, 1)
    return {"tokens": tokens, "cache_keys": cache_keys, "cache_values": cache_values, "joined_weight": joined_weight, "output_weight": output_weight, "upward_weight": upward_weight, "downward_weight": downward_weight, "first_gain": first_gain, "second_gain": second_gain, "bias_table": bias_table, "bucket_index": bucket_index, "cached_lengths": cached_lengths, "new_counts": new_counts, "extend_flags": extend_flags}


EPSILON = 1e-06
FLOOR_SCORE = -1e+30

def rms_rows(rows, gain):
    rows = rows.astype(jnp.float32)
    mean_square = lax.optimization_barrier(jnp.mean(rows * rows, axis=-1, keepdims=True))
    return (rows * lax.rsqrt(mean_square + EPSILON) * gain).astype(jnp.bfloat16)

def reference(tokens, cache_keys, cache_values, joined_weight, output_weight, upward_weight, downward_weight, first_gain, second_gain, bias_table, bucket_index, cached_lengths, new_counts, extend_flags):
    joined_half = joined_weight.astype(jnp.bfloat16)
    output_half = output_weight.astype(jnp.bfloat16)
    upward_half = upward_weight.astype(jnp.bfloat16)
    downward_half = downward_weight.astype(jnp.bfloat16)
    rel_bias = jnp.transpose(jnp.take(bias_table, bucket_index, axis=0))
    normed = rms_rows(tokens, first_gain)
    projected = jnp.dot(normed, joined_half, preferred_element_type=jnp.float32).astype(jnp.bfloat16)
    attn_width = HEADS * HEAD
    queries = projected[:, :attn_width].reshape(REQS, NEW, HEADS, HEAD)
    new_keys = projected[:, attn_width:2 * attn_width].reshape(REQS, NEW, HEADS, HEAD)
    new_values = projected[:, 2 * attn_width:].reshape(REQS, NEW, HEADS, HEAD)
    old_keys = cache_keys.reshape(REQS, CACHE_MAX, HEADS, HEAD)
    old_values = cache_values.reshape(REQS, CACHE_MAX, HEADS, HEAD)
    used_lengths = (cached_lengths * extend_flags).astype(jnp.int32)

    def one_request(packed):
        query_rows, key_new, value_new, key_old, value_old, used_len, new_count = packed
        cache_slots = jnp.arange(CACHE_MAX, dtype=jnp.int32)
        new_slots = jnp.arange(NEW, dtype=jnp.int32)
        key_pos = jnp.concatenate([cache_slots, used_len + new_slots])
        key_ok = jnp.concatenate([cache_slots < used_len, new_slots < new_count])
        query_pos = used_len + new_slots
        all_keys = jnp.concatenate([key_old, key_new], axis=0).astype(jnp.float32)
        all_values = jnp.concatenate([value_old, value_new], axis=0).astype(jnp.float32)
        scores = jnp.einsum('qhd,khd->hqk', query_rows.astype(jnp.float32), all_keys)
        offset = key_pos[None, :] - query_pos[:, None] + (SPAN - 1)
        scores = scores + jnp.take(rel_bias, offset, axis=1)
        allowed = key_ok[None, None, :]
        row_top = lax.optimization_barrier(jnp.max(jnp.where(allowed, scores, FLOOR_SCORE), axis=2, keepdims=True))
        weights = jnp.where(allowed, jnp.exp(scores - row_top), 0.0)
        row_total = lax.optimization_barrier(jnp.sum(weights, axis=2))
        rounded = lax.optimization_barrier(weights.astype(jnp.bfloat16)).astype(jnp.float32)
        mixed_rows = jnp.einsum('hqk,khd->qhd', rounded, all_values) / jnp.transpose(row_total)[:, :, None]
        return mixed_rows.reshape(NEW, attn_width).astype(jnp.bfloat16)
    attention = lax.map(one_request, (queries, new_keys, new_values, old_keys, old_values, used_lengths, new_counts))
    attention = attention.reshape(REQS * NEW, attn_width)
    attended = lax.dot_general(attention, output_half, (((1,), (1,)), ((), ())), preferred_element_type=jnp.float32)
    hidden = tokens.astype(jnp.float32) + attended
    normed_mid = rms_rows(hidden, second_gain)
    active = jax.nn.relu(jnp.dot(normed_mid, upward_half, preferred_element_type=jnp.float32)).astype(jnp.bfloat16)
    feed_out = lax.dot_general(active, downward_half, (((1,), (1,)), ((), ())), preferred_element_type=jnp.float32)
    return (hidden + feed_out).astype(jnp.bfloat16)
```

```python
import functools

import jax
import jax.numpy as jnp
from jax import lax
from jax.experimental import pallas as pl
from jax.experimental.pallas import tpu as pltpu
from jax.sharding import PartitionSpec as P

EPSILON = 1e-06
FLOOR_SCORE = -1e30
HALF = jnp.bfloat16
FULL = jnp.float32

VMEM = pl.BlockSpec(memory_space=pltpu.VMEM)
SMEM = pl.BlockSpec(memory_space=pltpu.SMEM)
ANY = pl.BlockSpec(memory_space=pl.ANY)


def params(megabytes):
    return pltpu.CompilerParams(vmem_limit_bytes=megabytes * 1024 * 1024)


def cost(flops, bytes_accessed):
    return pl.CostEstimate(flops=flops, bytes_accessed=bytes_accessed, transcendentals=0)


def swap(array, axis, mask):
    size = lax.axis_size(axis)
    return lax.ppermute(array, axis, [(i, i ^ mask) for i in range(size)])


def dot(left, right):
    return jnp.dot(left, right, preferred_element_type=FULL)


def dot_nt(left, right):
    return lax.dot_general(left, right, (((1,), (1,)), ((), ())), preferred_element_type=FULL)


def joined_kernel(ids, joined, *outs):
    mine = ids[0]
    ways = len(outs)
    width = outs[0].shape[1] // 3
    for k in range(ways):
        owner = mine ^ k
        for part in range(3):
            start = pl.multiple_of((part * ways + owner) * width, 128)
            outs[k][:, part * width : (part + 1) * width] = joined[:, pl.ds(start, width)].astype(HALF)


def forward_kernel(ids, output, upward, downward, *outs):
    mine = ids[0]
    ways = len(outs) // 2
    attn_width = output.shape[1]
    width = upward.shape[1] // ways
    output_half = output[...].astype(HALF)
    for k in range(ways):
        start = pl.multiple_of((mine ^ k) * width, 128)
        outs[k][:, :attn_width] = output_half
        outs[k][:, attn_width:] = upward[:, pl.ds(start, width)].astype(HALF)
        outs[ways + k][...] = downward[:, pl.ds(start, width)].astype(HALF)


def rms_rows(rows, gain):
    mean_square = jnp.mean(rows * rows, axis=-1, keepdims=True)
    return (rows * lax.rsqrt(mean_square + EPSILON) * gain).astype(HALF)


def prepare_kernel(ids, tokens, gain, table, buckets, normed, bias):
    used, count = ids[2], ids[3]
    normed[...] = rms_rows(tokens[...].astype(FULL), gain[...])
    heads, rows, keys = bias.shape
    cached = keys - rows
    spread = buckets.shape[1]
    hot = lax.broadcasted_iota(jnp.int32, (table.shape[0], spread), 0) == buckets[...]
    slots = lax.broadcasted_iota(jnp.int32, (rows, rows), 1)
    old_slots = lax.broadcasted_iota(jnp.int32, (rows, cached), 1)
    for h in range(heads):
        rel = jnp.sum(jnp.where(hot, table[:, h : h + 1], 0.0), axis=0, keepdims=True)
        rel = jnp.broadcast_to(rel, (8, spread))
        middle = spread // 2
        old_row = pltpu.roll(rel, used + (spread - (middle - rows)), 1)[:1, : rows + cached]
        new_row = rel[:1, middle - rows : middle + rows]
        old = jnp.broadcast_to(old_row, (rows, rows + cached))
        old = pltpu.roll(old, cached + 1, 1, stride=1, stride_axis=0)[:, :cached]
        new = jnp.broadcast_to(new_row, (rows, 2 * rows))
        new = pltpu.roll(new, rows + 1, 1, stride=1, stride_axis=0)[:, :rows]
        bias[h, :, :cached] = jnp.where(old_slots < used, old, FLOOR_SCORE)
        bias[h, :, cached:] = jnp.where(slots < count, new, FLOOR_SCORE)


def gather_copies(ids, sources, target, sems, columns=None):
    copies = []
    if len(sources) == 1:
        copies.append(pltpu.make_async_copy(sources[0], target, sems.at[0]))
        return copies
    mine, place = ids[0], ids[1]
    for j, source in enumerate(sources):
        for k in range(source.shape[0]):
            piece = source.at[k] if columns is None else source.at[k, :, columns]
            copies.append(
                pltpu.make_async_copy(
                    piece, target.at[place ^ j, mine ^ k], sems.at[j * source.shape[0] + k]
                )
            )
    return copies


def attend_kernel(pieces, ids, normed, old_keys, old_values, bias, *refs):
    sources, (out, weight, sems) = refs[:pieces], refs[pieces:]
    copies = gather_copies(ids, sources, weight, sems)
    for copy in copies:
        copy.start()
    for copy in copies:
        copy.wait()
    rows, features = normed.shape
    heads = bias.shape[0]
    width = out.shape[1]
    size = width // heads
    projected = dot(normed[...], weight[...].reshape(features, 3 * width)).astype(HALF)
    queries = projected[:, :width]
    new_keys = projected[:, width : 2 * width]
    new_values = projected[:, 2 * width :]
    cached = old_keys.shape[0]
    lanes = lax.broadcasted_iota(jnp.int32, (rows, width), 1)
    result = jnp.zeros((rows, width), FULL)
    for h in range(heads):
        inside = (lanes >= h * size) & (lanes < (h + 1) * size)
        query = jnp.where(inside, queries, jnp.zeros_like(queries))
        old = dot_nt(query, old_keys[...]) + bias[h, :, :cached]
        new = dot_nt(query, new_keys) + bias[h, :, cached:]
        top = jnp.maximum(
            jnp.max(old, axis=1, keepdims=True), jnp.max(new, axis=1, keepdims=True)
        )
        old = jnp.exp(old - top)
        new = jnp.exp(new - top)
        total = jnp.sum(old, axis=1, keepdims=True) + jnp.sum(new, axis=1, keepdims=True)
        mixed = dot(old.astype(HALF), old_values[...]) + dot(new.astype(HALF), new_values)
        result = jnp.where(inside, mixed / total, result)
    out[...] = result.astype(HALF)


def layer_kernel(pieces, ways, ids, tokens, gain, *refs):
    attended, refs = refs[:ways], refs[ways:]
    first, refs = refs[:pieces], refs[pieces:]
    second, refs = refs[:pieces], refs[pieces:]
    own, sends, refs = refs[0], refs[1:ways], refs[ways:]
    first_weight, second_weight, attention, feed, first_sems, second_sems = refs
    mine = ids[0]
    first_copies = gather_copies(ids, first, first_weight, first_sems)
    second_copies = gather_copies(ids, second, second_weight, second_sems)
    for copy in first_copies + second_copies:
        copy.start()
    rows, features = tokens.shape
    width = attended[0].shape[1]
    hidden_units = second_weight.shape[-1]
    for k in range(ways):
        start = pl.multiple_of((mine ^ k) * width, 128)
        attention[:, pl.ds(start, width)] = attended[k][...]
    for copy in first_copies:
        copy.wait()
    weight = first_weight[...].reshape(features, ways * width + hidden_units)
    hidden = tokens[...].astype(FULL) + dot_nt(attention[...], weight[:, : ways * width])
    inner = dot(rms_rows(hidden, gain[...]), weight[:, ways * width :])
    active = jnp.maximum(inner, 0.0).astype(HALF)
    for copy in second_copies:
        copy.wait()
    feed[0] = hidden
    feed[1] = dot_nt(active, second_weight[...].reshape(features, hidden_units))
    share = rows // ways
    for k in range(ways):
        start = pl.multiple_of((mine ^ k) * share, 8)
        if k == 0:
            own[...] = feed[0, pl.ds(start, share), :] + feed[1, pl.ds(start, share), :]
        else:
            sends[k - 1][...] = feed[1, pl.ds(start, share), :].astype(HALF)


def exchange(blocks):
    return [blocks[0]] + [swap(block, "tensor", k) for k, block in enumerate(blocks) if k]


def natural_gather(blocks):
    ways = len(blocks)
    mine = lax.axis_index("tensor")
    rows = jnp.concatenate([lax.select_n(mine ^ p, *blocks) for p in range(ways)])
    return [lax.all_gather(rows, "seq", axis=0, tiled=True)]


def plane_gather(blocks, near, far):
    block = jnp.stack(blocks)
    near_block = swap(block, "seq", near)
    far_block = swap(block, "seq", far)
    both_block = swap(near_block, "seq", far)
    held = {0: block, near: near_block, far: far_block, near | far: both_block}
    for j in (0, near, far, near | far):
        held[j | 1] = swap(held[j], "seq", 1)
    return [held[j] for j in range(8)]


def shards(
    tokens,
    cache_keys,
    cache_values,
    joined_weight,
    output_weight,
    upward_weight,
    downward_weight,
    first_gain,
    second_gain,
    bias_table,
    bucket_index,
    cached_lengths,
    new_counts,
    extend_flags,
):
    ways = lax.axis_size("tensor")
    places = lax.axis_size("seq")
    mine = lax.axis_index("tensor")
    place = lax.axis_index("seq")
    rows, features = tokens.shape
    cached = cache_keys.shape[0]
    heads = bias_table.shape[1]
    width = cache_keys.shape[1]
    trainer_rows = joined_weight.shape[0]
    hidden_units = upward_weight.shape[1] // ways
    attn_width = output_weight.shape[1]
    span = bucket_index.shape[0] + 1
    by_swaps = places == 8
    used = cached_lengths[place] * extend_flags[place]
    ids = jnp.stack([mine, place, used, new_counts[place]]).astype(jnp.int32)

    joined_blocks = pl.pallas_call(
        joined_kernel,
        name="cut_joined",
        out_shape=[jax.ShapeDtypeStruct((trainer_rows, 3 * width), HALF)] * ways,
        in_specs=[SMEM, VMEM],
        out_specs=[VMEM] * ways,
        compiler_params=params(16),
    )(ids, joined_weight)
    joined_blocks = exchange(joined_blocks)
    forward_blocks = pl.pallas_call(
        forward_kernel,
        name="cut_forward",
        out_shape=[jax.ShapeDtypeStruct((trainer_rows, attn_width + hidden_units), HALF)] * ways
        + [jax.ShapeDtypeStruct((trainer_rows, hidden_units), HALF)] * ways,
        in_specs=[SMEM, VMEM, VMEM, VMEM],
        out_specs=[VMEM] * (2 * ways),
        compiler_params=params(16),
    )(ids, output_weight, upward_weight, downward_weight)
    first_blocks = exchange(forward_blocks[:ways])
    second_blocks = exchange(forward_blocks[ways:])

    normed, bias = pl.pallas_call(
        prepare_kernel,
        name="prepare",
        out_shape=[
            jax.ShapeDtypeStruct((rows, features), HALF),
            jax.ShapeDtypeStruct((heads, rows, cached + rows), FULL),
        ],
        in_specs=[SMEM, VMEM, VMEM, VMEM, VMEM],
        out_specs=[VMEM, VMEM],
        compiler_params=params(24),
        cost_estimate=cost(10**8, 4 * 10**6),
    )(
        ids,
        tokens,
        first_gain.reshape(1, features),
        bias_table,
        jnp.pad(bucket_index, (0, 1)).reshape(1, span),
    )

    if by_swaps:
        joined_all = plane_gather(joined_blocks, 4, 2)
        first_all = plane_gather(first_blocks, 2, 4)
        second_all = plane_gather(second_blocks, 4, 2)
        lead = (places, ways, trainer_rows)
    else:
        joined_all = natural_gather(joined_blocks)
        first_all = natural_gather(first_blocks)
        second_all = natural_gather(second_blocks)
        lead = (features,)
    pieces = len(joined_all)
    sems = pltpu.SemaphoreType.DMA((pieces * ways,))

    attention = pl.pallas_call(
        functools.partial(attend_kernel, pieces),
        name="attend",
        out_shape=jax.ShapeDtypeStruct((rows, width), HALF),
        in_specs=[SMEM, VMEM, VMEM, VMEM, VMEM] + [ANY] * pieces,
        out_specs=VMEM,
        scratch_shapes=[pltpu.VMEM(lead + (3 * width,), HALF), sems],
        compiler_params=params(24),
        cost_estimate=cost(10**9, 6 * 10**6),
    )(ids, normed, cache_keys, cache_values, bias, *joined_all)

    attended = [attention] + [swap(attention, "tensor", k) for k in range(1, ways)]
    share = rows // ways
    own, *sends = pl.pallas_call(
        functools.partial(layer_kernel, pieces, ways),
        name="layer",
        out_shape=[jax.ShapeDtypeStruct((share, features), FULL)]
        + [jax.ShapeDtypeStruct((share, features), HALF)] * (ways - 1),
        in_specs=[SMEM, VMEM, VMEM] + [VMEM] * ways + [ANY] * (2 * pieces),
        out_specs=[VMEM] * ways,
        scratch_shapes=[
            pltpu.VMEM(lead + (attn_width + hidden_units,), HALF),
            pltpu.VMEM(lead + (hidden_units,), HALF),
            pltpu.VMEM((rows, attn_width), HALF),
            pltpu.VMEM((2, rows, features), FULL),
            sems,
            sems,
        ],
        compiler_params=params(32),
        cost_estimate=cost(2 * 10**9, 8 * 10**6),
    )(ids, tokens, second_gain.reshape(1, features), *attended, *first_all, *second_all)

    total = own
    for k, send in enumerate(sends, 1):
        total = total + swap(send, "tensor", k).astype(FULL)
    return total.astype(HALF)


def solution(mesh):
    return jax.shard_map(
        shards,
        mesh=mesh,
        in_specs=(
            P("seq", None),
            P("seq", "tensor"),
            P("seq", "tensor"),
            P(("seq", "tensor"), None),
            P(("seq", "tensor"), None),
            P(("seq", "tensor"), None),
            P(("seq", "tensor"), None),
            P(),
            P(),
            P(None, "tensor"),
            P(),
            P(),
            P(),
            P(),
        ),
        out_specs=P(("seq", "tensor"), None),
        check_vma=False,
    )
```

```python
import functools

import jax
import jax.numpy as jnp
from jax import lax
from jax.experimental import pallas as pl
from jax.experimental.pallas import tpu as pltpu
from jax.sharding import PartitionSpec as P

EPSILON = 1e-06
FLOOR_SCORE = -1e30
HALF = jnp.bfloat16
FULL = jnp.float32
VMEM_GRANT = 60
ATTEND_COST = 2 * 10**10

VMEM = pl.BlockSpec(memory_space=pltpu.VMEM)
SMEM = pl.BlockSpec(memory_space=pltpu.SMEM)
HBM = pl.BlockSpec(memory_space=pltpu.HBM)
ANY = pl.BlockSpec(memory_space=pl.ANY)


def params(megabytes):
    return pltpu.CompilerParams(vmem_limit_bytes=megabytes * 1024 * 1024)


def cost(flops, bytes_accessed):
    return pl.CostEstimate(flops=flops, bytes_accessed=bytes_accessed, transcendentals=0)


def swap(array, axis, mask):
    size = lax.axis_size(axis)
    return lax.ppermute(array, axis, [(i, i ^ mask) for i in range(size)])


def dot(left, right):
    return jnp.dot(left, right, preferred_element_type=FULL)


def dot_nt(left, right):
    return lax.dot_general(left, right, (((1,), (1,)), ((), ())), preferred_element_type=FULL)


def here():
    return lax.axis_index("tensor"), lax.axis_index("seq")


def load(sources, targets, sems):
    copies = [
        pltpu.make_async_copy(source, target, sems.at[i])
        for i, (source, target) in enumerate(zip(sources, targets))
    ]
    for copy in copies:
        copy.start()
    for copy in copies:
        copy.wait()


def joined_kernel(joined_source, *refs):
    outs, (joined, sems) = refs[:-2], refs[-2:]
    load([joined_source], [joined], sems)
    mine, _ = here()
    ways = len(outs)
    width = outs[0].shape[1] // 3
    for k in range(ways):
        owner = mine ^ k
        for part in range(3):
            start = pl.multiple_of((part * ways + owner) * width, 128)
            outs[k][:, part * width : (part + 1) * width] = joined[:, pl.ds(start, width)].astype(HALF)


def forward_kernel(*refs):
    sources, (blocks, output, upward, downward, sems) = refs[-8:-5], refs[-5:]
    load(sources, [output, upward, downward], sems)
    ways = blocks.shape[0]
    whole = output.shape[1]
    width = upward.shape[1] // ways
    output_half = output[...].astype(HALF)
    for t in range(ways):
        blocks[t, :, :whole] = output_half
        blocks[t, :, whole : whole + width] = upward[:, t * width : (t + 1) * width].astype(HALF)
        blocks[t, :, whole + width :] = downward[:, t * width : (t + 1) * width].astype(HALF)


def rms_rows(rows, gain):
    mean_square = jnp.mean(rows * rows, axis=-1, keepdims=True)
    return (rows * lax.rsqrt(mean_square + EPSILON) * gain).astype(HALF)


def prepare_kernel(after, lengths, flags, counts, tokens, gain, table, buckets, normed, bias, *refs):
    numbers, padded, sems = refs
    load([lengths, flags, counts], [numbers.at[i] for i in range(3)], sems)
    _, place = here()
    used = numbers[0, place] * numbers[1, place]
    count = numbers[2, place]
    padded[...] = jnp.zeros_like(padded)
    padded[:, : buckets.shape[1]] = buckets[...]
    normed[...] = rms_rows(tokens[...].astype(FULL), gain[...])
    heads, rows, keys = bias.shape
    cached = keys - rows
    spread = padded.shape[1]
    hot = lax.broadcasted_iota(jnp.int32, (table.shape[1], spread), 0) == padded[...]
    rows_of_heads = jnp.dot(
        table[...],
        hot.astype(FULL),
        precision=lax.Precision.HIGHEST,
        preferred_element_type=FULL,
    )
    slots = lax.broadcasted_iota(jnp.int32, (rows, rows), 1)
    old_slots = lax.broadcasted_iota(jnp.int32, (rows, cached), 1)
    for h in range(heads):
        rel = jnp.broadcast_to(rows_of_heads[h : h + 1], (8, spread))
        middle = spread // 2
        old_row = pltpu.roll(rel, used + (spread - (middle - rows)), 1)[:1, : rows + cached]
        new_row = rel[:1, middle - rows : middle + rows]
        old = jnp.broadcast_to(old_row, (rows, rows + cached))
        old = pltpu.roll(old, cached + 1, 1, stride=1, stride_axis=0)[:, :cached]
        new = jnp.broadcast_to(new_row, (rows, 2 * rows))
        new = pltpu.roll(new, rows + 1, 1, stride=1, stride_axis=0)[:, :rows]
        bias[h, :, :cached] = jnp.where(old_slots < used, old, FLOOR_SCORE)
        bias[h, :, cached:] = jnp.where(slots < count, new, FLOOR_SCORE)


def stack_kernel(ways, *refs):
    target, sems = refs[-2:]
    mine, _ = here()
    load(refs[:ways], [target.at[mine ^ k] for k in range(ways)], sems)


def stack(blocks, *after):
    ways = len(blocks)
    return pl.pallas_call(
        functools.partial(stack_kernel, ways),
        name="stack",
        out_shape=jax.ShapeDtypeStruct((ways,) + blocks[0].shape, HALF),
        in_specs=[HBM] * ways + [ANY] * len(after),
        out_specs=VMEM,
        scratch_shapes=[pltpu.SemaphoreType.DMA((ways,))],
        compiler_params=params(VMEM_GRANT),
    )(*blocks, *after)


def gather_copies(pieces, sources, start, target, sems):
    width = target.shape[-1]
    if len(sources) == 1:
        source = sources[0].at[:, start : start + width]
        return [pltpu.make_async_copy(source, target, sems.at[0])]
    _, place = here()
    copies = []
    for i, ((j, t), source) in enumerate(zip(pieces, sources)):
        block = target.at[place ^ j, t : t + source.shape[0]]
        source = source.at[:, :, start : start + width]
        copies.append(pltpu.make_async_copy(source, block, sems.at[i]))
    return copies


def attend_kernel(pieces, normed, old_keys, old_values, bias, *refs):
    sources, (out, weight, sems) = refs[: len(pieces)], refs[len(pieces) :]
    copies = gather_copies(pieces, sources, 0, weight, sems)
    for copy in copies:
        copy.start()
    for copy in copies:
        copy.wait()
    rows, features = normed.shape
    heads = bias.shape[0]
    width = out.shape[1]
    size = width // heads
    projected = dot(normed[...], weight[...].reshape(features, 3 * width)).astype(HALF)
    queries = projected[:, :width]
    new_keys = projected[:, width : 2 * width]
    new_values = projected[:, 2 * width :]
    cached = old_keys.shape[0]
    lanes = lax.broadcasted_iota(jnp.int32, (rows, width), 1)
    result = jnp.zeros((rows, width), FULL)
    for h in range(heads):
        inside = (lanes >= h * size) & (lanes < (h + 1) * size)
        query = jnp.where(inside, queries, jnp.zeros_like(queries))
        old = dot_nt(query, old_keys[...]) + bias[h, :, :cached]
        new = dot_nt(query, new_keys) + bias[h, :, cached:]
        top = jnp.maximum(
            jnp.max(old, axis=1, keepdims=True), jnp.max(new, axis=1, keepdims=True)
        )
        old = jnp.exp(old - top)
        new = jnp.exp(new - top)
        total = jnp.sum(old, axis=1, keepdims=True) + jnp.sum(new, axis=1, keepdims=True)
        mixed = dot(old.astype(HALF), old_values[...]) + dot(new.astype(HALF), new_values)
        result = jnp.where(inside, mixed / total, result)
    out[...] = result.astype(HALF)


def layer_kernel(pieces, ways, tokens, gain, *refs):
    attended, refs = refs[:ways], refs[ways:]
    sources, refs = refs[: len(pieces)], refs[len(pieces) :]
    outs, (output, upward, downward, attention, hidden, feed, sems) = refs[:ways], refs[ways:]
    features = tokens.shape[1]
    copies, start = [], 0
    for i, weight in enumerate((output, upward, downward)):
        copies.append(gather_copies(pieces, sources, start, weight, sems.at[i]))
        start += weight.shape[-1]
        for copy in copies[-1]:
            copy.start()
    mine, _ = here()
    width = attended[0].shape[1]
    for k in range(ways):
        attention[:, pl.ds(pl.multiple_of((mine ^ k) * width, 128), width)] = attended[k][...]

    def arrived(i, weight):
        for copy in copies[i]:
            copy.wait()
        return weight[...].reshape(features, -1)

    hidden[...] = tokens[...].astype(FULL) + dot_nt(attention[...], arrived(0, output))
    inner = dot(rms_rows(hidden[...], gain[...]), arrived(1, upward))
    active = jnp.maximum(inner, 0.0).astype(HALF)
    feed[...] = dot_nt(active, arrived(2, downward))
    share = tokens.shape[0] // ways
    for k in range(ways):
        rows_of = pl.ds(pl.multiple_of((mine ^ k) * share, 8), share)
        if k == 0:
            outs[0][...] = hidden[rows_of, :] + feed[rows_of, :]
        else:
            outs[k][...] = feed[rows_of, :].astype(HALF)


def exchange(blocks):
    return [blocks[0]] + [swap(block, "tensor", k) for k, block in enumerate(blocks) if k]


def natural_gather(rows):
    return lax.all_gather(rows.reshape(-1, rows.shape[-1]), "seq", axis=0, tiled=True)


def together(*arrays):
    return lax.optimization_barrier(arrays)


NEAR, FAR = 4, 2


def first_hops(block):
    return together(swap(block, "seq", NEAR), swap(block, "seq", FAR))


def with_cores(held):
    for (j, t), piece in list(held.items()):
        held[j | 1, t] = swap(piece, "seq", 1)
    return list(held), list(held.values())


def whole_hop(block, near, far):
    held = {(0, 0): block, (NEAR, 0): near, (FAR, 0): far}
    held[NEAR | FAR, 0] = swap(near, "seq", FAR)
    return held


def half_hops(block, near, far):
    half = block.shape[0] // 2
    held = {(0, 0): block, (NEAR, 0): near, (FAR, 0): far}
    held[NEAR | FAR, 0] = swap(near[:half], "seq", FAR)
    held[NEAR | FAR, half] = swap(far[half:], "seq", NEAR)
    return held


def owners_blocks(blocks):
    return lax.all_to_all(blocks, "tensor", split_axis=0, concat_axis=0, tiled=True)


def shards(
    tokens,
    cache_keys,
    cache_values,
    joined_weight,
    output_weight,
    upward_weight,
    downward_weight,
    first_gain,
    second_gain,
    bias_table,
    bucket_index,
    cached_lengths,
    new_counts,
    extend_flags,
):
    ways = lax.axis_size("tensor")
    places = lax.axis_size("seq")
    mine = lax.axis_index("tensor")
    rows, features = tokens.shape
    cached = cache_keys.shape[0]
    heads = bias_table.shape[1]
    width = cache_keys.shape[1]
    trainer_rows = joined_weight.shape[0]
    hidden_units = upward_weight.shape[1] // ways
    attn_width = output_weight.shape[1]
    columns = attn_width + 2 * hidden_units
    span = bucket_index.shape[0] + 1

    joined_blocks = pl.pallas_call(
        joined_kernel,
        name="cut_joined",
        out_shape=[jax.ShapeDtypeStruct((trainer_rows, 3 * width), HALF)] * ways,
        in_specs=[HBM],
        out_specs=[VMEM] * ways,
        scratch_shapes=[
            pltpu.VMEM(joined_weight.shape, FULL),
            pltpu.SemaphoreType.DMA((1,)),
        ],
        compiler_params=params(VMEM_GRANT),
    )(joined_weight)
    forward = pl.pallas_call(
        forward_kernel,
        name="cut_forward",
        out_shape=jax.ShapeDtypeStruct((ways, trainer_rows, columns), HALF),
        in_specs=[ANY, HBM, HBM, HBM],
        out_specs=VMEM,
        scratch_shapes=[
            pltpu.VMEM(weight.shape, FULL)
            for weight in (output_weight, upward_weight, downward_weight)
        ]
        + [pltpu.SemaphoreType.DMA((3,))],
        compiler_params=params(VMEM_GRANT),
    )(joined_blocks[0], output_weight, upward_weight, downward_weight)
    own_joined, joined_blocks = joined_blocks[0], exchange(joined_blocks)

    normed, bias = pl.pallas_call(
        prepare_kernel,
        name="prepare",
        out_shape=[
            jax.ShapeDtypeStruct((rows, features), HALF),
            jax.ShapeDtypeStruct((heads, rows, cached + rows), FULL),
        ],
        in_specs=[ANY, HBM, HBM, HBM, VMEM, VMEM, VMEM, VMEM],
        out_specs=[VMEM, VMEM],
        scratch_shapes=[
            pltpu.SMEM((3,) + new_counts.shape, jnp.int32),
            pltpu.VMEM((1, span), jnp.int32),
            pltpu.SemaphoreType.DMA((3,)),
        ],
        compiler_params=params(VMEM_GRANT),
        cost_estimate=cost(10**8, 4 * 10**6),
    )(
        own_joined,
        cached_lengths,
        extend_flags,
        new_counts,
        tokens,
        first_gain.reshape(1, features),
        bias_table.T,
        bucket_index.reshape(1, span - 1),
    )

    if places == 8:
        lead = (places, ways, trainer_rows)
        joined = stack(joined_blocks, normed, forward)
        forward, joined = together(forward, joined)
        held = whole_hop(joined, *first_hops(joined))
        joined_pieces, joined_all = with_cores(held)
    else:
        lead = (features,)
        natural = [lax.select_n(mine ^ t, *joined_blocks) for t in range(ways)]
        joined_pieces, joined_all = [None], [natural_gather(jnp.stack(natural))]
    forward = owners_blocks(forward)

    attention = pl.pallas_call(
        functools.partial(attend_kernel, joined_pieces),
        name="attend",
        out_shape=jax.ShapeDtypeStruct((rows, width), HALF),
        in_specs=[VMEM, VMEM, VMEM, VMEM] + [ANY] * len(joined_all),
        out_specs=VMEM,
        scratch_shapes=[pltpu.VMEM(lead + (3 * width,), HALF), pltpu.SemaphoreType.DMA((8,))],
        compiler_params=params(VMEM_GRANT),
        cost_estimate=cost(ATTEND_COST, 6 * 10**6),
    )(normed, cache_keys, cache_values, bias, *joined_all)

    attended = [attention] + [swap(attention, "tensor", k) for k in range(1, ways)]
    if places == 8:
        forward_pieces, forward_all = with_cores(half_hops(forward, *first_hops(forward)))
    else:
        forward_pieces, forward_all = [None], [natural_gather(forward)]
    share = rows // ways
    own, *sends = pl.pallas_call(
        functools.partial(layer_kernel, forward_pieces, ways),
        name="layer",
        out_shape=[jax.ShapeDtypeStruct((share, features), FULL)]
        + [jax.ShapeDtypeStruct((share, features), HALF)] * (ways - 1),
        in_specs=[VMEM, VMEM] + [VMEM] * ways + [ANY] * len(forward_all),
        out_specs=[VMEM] * ways,
        scratch_shapes=[
            pltpu.VMEM(lead + (attn_width,), HALF),
            pltpu.VMEM(lead + (hidden_units,), HALF),
            pltpu.VMEM(lead + (hidden_units,), HALF),
            pltpu.VMEM((rows, attn_width), HALF),
            pltpu.VMEM((rows, features), FULL),
            pltpu.VMEM((rows, features), FULL),
            pltpu.SemaphoreType.DMA((3, len(forward_all))),
        ],
        compiler_params=params(VMEM_GRANT),
        cost_estimate=cost(2 * 10**9, 8 * 10**6),
    )(tokens, second_gain.reshape(1, features), *attended, *forward_all)

    total = own
    for k, send in enumerate(sends, 1):
        total = total + swap(send, "tensor", k).astype(FULL)
    return total.astype(HALF)


def solution(mesh):
    return jax.shard_map(
        shards,
        mesh=mesh,
        in_specs=(
            P("seq", None),
            P("seq", "tensor"),
            P("seq", "tensor"),
            P(("seq", "tensor"), None),
            P(("seq", "tensor"), None),
            P(("seq", "tensor"), None),
            P(("seq", "tensor"), None),
            P(),
            P(),
            P(None, "tensor"),
            P(),
            P(),
            P(),
            P(),
        ),
        out_specs=P(("seq", "tensor"), None),
        check_vma=False,
    )
```

```python
import functools

import jax
import jax.numpy as jnp
from jax import lax
from jax.experimental import pallas as pl
from jax.experimental.pallas import tpu as pltpu
from jax.sharding import PartitionSpec as P

EPSILON = 1e-06
FLOOR_SCORE = -1e30
HALF = jnp.bfloat16
FULL = jnp.float32
VMEM_GRANT = 32
ATTEND_COST = 2 * 10**10

VMEM = pl.BlockSpec(memory_space=pltpu.VMEM)
SMEM = pl.BlockSpec(memory_space=pltpu.SMEM)
HBM = pl.BlockSpec(memory_space=pltpu.HBM)
ANY = pl.BlockSpec(memory_space=pl.ANY)


def params(megabytes):
    return pltpu.CompilerParams(vmem_limit_bytes=megabytes * 1024 * 1024)


def cost(flops, bytes_accessed):
    return pl.CostEstimate(flops=flops, bytes_accessed=bytes_accessed, transcendentals=0)


def swap(array, axis, mask):
    size = lax.axis_size(axis)
    return lax.ppermute(array, axis, [(i, i ^ mask) for i in range(size)])


def dot(left, right):
    return jnp.dot(left, right, preferred_element_type=FULL)


def dot_nt(left, right):
    return lax.dot_general(left, right, (((1,), (1,)), ((), ())), preferred_element_type=FULL)


def here():
    return lax.axis_index("tensor"), lax.axis_index("seq")


def load(sources, targets, sems):
    copies = [
        pltpu.make_async_copy(source, target, sems.at[i])
        for i, (source, target) in enumerate(zip(sources, targets))
    ]
    for copy in copies:
        copy.start()
    for copy in copies:
        copy.wait()


def joined_kernel(joined_source, *refs):
    outs, (joined, sems) = refs[:-2], refs[-2:]
    load([joined_source], [joined], sems)
    mine, _ = here()
    ways = len(outs)
    width = outs[0].shape[1] // 3
    for k in range(ways):
        owner = mine ^ k
        for part in range(3):
            start = pl.multiple_of((part * ways + owner) * width, 128)
            outs[k][:, part * width : (part + 1) * width] = joined[:, pl.ds(start, width)].astype(HALF)


def forward_kernel(*refs):
    sources, (blocks, output, upward, downward, sems) = refs[-8:-5], refs[-5:]
    load(sources, [output, upward, downward], sems)
    ways = blocks.shape[0]
    whole = output.shape[1]
    width = upward.shape[1] // ways
    output_half = output[...].astype(HALF)
    for t in range(ways):
        blocks[t, :, :whole] = output_half
        blocks[t, :, whole : whole + width] = upward[:, t * width : (t + 1) * width].astype(HALF)
        blocks[t, :, whole + width :] = downward[:, t * width : (t + 1) * width].astype(HALF)


def rms_rows(rows, gain):
    mean_square = jnp.mean(rows * rows, axis=-1, keepdims=True)
    return (rows * lax.rsqrt(mean_square + EPSILON) * gain).astype(HALF)


def prepare_kernel(after, lengths, flags, counts, tokens, gain, table, buckets, normed, bias, *refs):
    numbers, padded, sems = refs
    load([lengths, flags, counts], [numbers.at[i] for i in range(3)], sems)
    _, place = here()
    used = numbers[0, place] * numbers[1, place]
    count = numbers[2, place]
    padded[...] = jnp.zeros_like(padded)
    padded[:, : buckets.shape[1]] = buckets[...]
    normed[...] = rms_rows(tokens[...].astype(FULL), gain[...])
    heads, rows, keys = bias.shape
    cached = keys - rows
    spread = padded.shape[1]
    hot = lax.broadcasted_iota(jnp.int32, (table.shape[1], spread), 0) == padded[...]
    rows_of_heads = jnp.dot(
        table[...],
        hot.astype(FULL),
        precision=lax.Precision.HIGHEST,
        preferred_element_type=FULL,
    )
    slots = lax.broadcasted_iota(jnp.int32, (rows, rows), 1)
    old_slots = lax.broadcasted_iota(jnp.int32, (rows, cached), 1)
    for h in range(heads):
        rel = jnp.broadcast_to(rows_of_heads[h : h + 1], (8, spread))
        middle = spread // 2
        old_row = pltpu.roll(rel, used + (spread - (middle - rows)), 1)[:1, : rows + cached]
        new_row = rel[:1, middle - rows : middle + rows]
        old = jnp.broadcast_to(old_row, (rows, rows + cached))
        old = pltpu.roll(old, cached + 1, 1, stride=1, stride_axis=0)[:, :cached]
        new = jnp.broadcast_to(new_row, (rows, 2 * rows))
        new = pltpu.roll(new, rows + 1, 1, stride=1, stride_axis=0)[:, :rows]
        bias[h, :, :cached] = jnp.where(old_slots < used, old, FLOOR_SCORE)
        bias[h, :, cached:] = jnp.where(slots < count, new, FLOOR_SCORE)


def stack_kernel(ways, *refs):
    target, sems = refs[-2:]
    mine, _ = here()
    load(refs[:ways], [target.at[mine ^ k] for k in range(ways)], sems)


def stack(blocks, *after):
    ways = len(blocks)
    return pl.pallas_call(
        functools.partial(stack_kernel, ways),
        name="stack",
        out_shape=jax.ShapeDtypeStruct((ways,) + blocks[0].shape, HALF),
        in_specs=[HBM] * ways + [ANY] * len(after),
        out_specs=VMEM,
        scratch_shapes=[pltpu.SemaphoreType.DMA((ways,))],
        compiler_params=params(VMEM_GRANT),
    )(*blocks, *after)


def gather_copies(pieces, sources, start, target, sems):
    width = target.shape[-1]
    if len(sources) == 1:
        source = sources[0].at[:, start : start + width]
        return [pltpu.make_async_copy(source, target, sems.at[0])]
    _, place = here()
    copies = []
    for i, ((j, t), source) in enumerate(zip(pieces, sources)):
        block = target.at[place ^ j, t : t + source.shape[0]]
        source = source.at[:, :, start : start + width]
        copies.append(pltpu.make_async_copy(source, block, sems.at[i]))
    return copies


def attend_kernel(pieces, normed, old_keys, old_values, bias, *refs):
    sources, (out, weight, sems) = refs[: len(pieces)], refs[len(pieces) :]
    copies = gather_copies(pieces, sources, 0, weight, sems)
    for copy in copies:
        copy.start()
    for copy in copies:
        copy.wait()
    rows, features = normed.shape
    heads = bias.shape[0]
    width = out.shape[1]
    size = width // heads
    projected = dot(normed[...], weight[...].reshape(features, 3 * width)).astype(HALF)
    queries = projected[:, :width]
    new_keys = projected[:, width : 2 * width]
    new_values = projected[:, 2 * width :]
    cached = old_keys.shape[0]
    lanes = lax.broadcasted_iota(jnp.int32, (rows, width), 1)
    result = jnp.zeros((rows, width), FULL)
    for h in range(heads):
        inside = (lanes >= h * size) & (lanes < (h + 1) * size)
        query = jnp.where(inside, queries, jnp.zeros_like(queries))
        old = dot_nt(query, old_keys[...]) + bias[h, :, :cached]
        new = dot_nt(query, new_keys) + bias[h, :, cached:]
        top = jnp.maximum(
            jnp.max(old, axis=1, keepdims=True), jnp.max(new, axis=1, keepdims=True)
        )
        old = jnp.exp(old - top)
        new = jnp.exp(new - top)
        total = jnp.sum(old, axis=1, keepdims=True) + jnp.sum(new, axis=1, keepdims=True)
        mixed = dot(old.astype(HALF), old_values[...]) + dot(new.astype(HALF), new_values)
        result = jnp.where(inside, mixed / total, result)
    out[...] = result.astype(HALF)


def layer_kernel(pieces, ways, tokens, gain, *refs):
    attended, refs = refs[:ways], refs[ways:]
    sources, refs = refs[: len(pieces)], refs[len(pieces) :]
    outs, (output, upward, downward, attention, hidden, feed, sems) = refs[:ways], refs[ways:]
    features = tokens.shape[1]
    copies, start = [], 0
    for i, weight in enumerate((output, upward, downward)):
        copies.append(gather_copies(pieces, sources, start, weight, sems.at[i]))
        start += weight.shape[-1]
        for copy in copies[-1]:
            copy.start()
    mine, _ = here()
    width = attended[0].shape[1]
    for k in range(ways):
        attention[:, pl.ds(pl.multiple_of((mine ^ k) * width, 128), width)] = attended[k][...]

    def arrived(i, weight):
        for copy in copies[i]:
            copy.wait()
        return weight[...].reshape(features, -1)

    hidden[...] = tokens[...].astype(FULL) + dot_nt(attention[...], arrived(0, output))
    inner = dot(rms_rows(hidden[...], gain[...]), arrived(1, upward))
    active = jnp.maximum(inner, 0.0).astype(HALF)
    feed[...] = dot_nt(active, arrived(2, downward))
    share = tokens.shape[0] // ways
    for k in range(ways):
        rows_of = pl.ds(pl.multiple_of((mine ^ k) * share, 8), share)
        if k == 0:
            outs[0][...] = hidden[rows_of, :] + feed[rows_of, :]
        else:
            outs[k][...] = feed[rows_of, :].astype(HALF)


def exchange(blocks):
    return [blocks[0]] + [swap(block, "tensor", k) for k, block in enumerate(blocks) if k]


def natural_gather(rows):
    return lax.all_gather(rows.reshape(-1, rows.shape[-1]), "seq", axis=0, tiled=True)


def together(*arrays):
    return lax.optimization_barrier(arrays)


NEAR, FAR = 4, 2


def first_hops(block):
    return together(swap(block, "seq", NEAR), swap(block, "seq", FAR))


def with_cores(held):
    for (j, t), piece in list(held.items()):
        held[j | 1, t] = swap(piece, "seq", 1)
    return list(held), list(held.values())


def whole_hop(block, near, far):
    held = {(0, 0): block, (NEAR, 0): near, (FAR, 0): far}
    held[NEAR | FAR, 0] = swap(near, "seq", FAR)
    return held


def half_hops(block, near, far):
    half = block.shape[0] // 2
    held = {(0, 0): block, (NEAR, 0): near, (FAR, 0): far}
    held[NEAR | FAR, 0] = swap(near[:half], "seq", FAR)
    held[NEAR | FAR, half] = swap(far[half:], "seq", NEAR)
    return held


def owners_blocks(blocks):
    return lax.all_to_all(blocks, "tensor", split_axis=0, concat_axis=0, tiled=True)


def shards(
    tokens,
    cache_keys,
    cache_values,
    joined_weight,
    output_weight,
    upward_weight,
    downward_weight,
    first_gain,
    second_gain,
    bias_table,
    bucket_index,
    cached_lengths,
    new_counts,
    extend_flags,
):
    ways = lax.axis_size("tensor")
    places = lax.axis_size("seq")
    mine = lax.axis_index("tensor")
    rows, features = tokens.shape
    cached = cache_keys.shape[0]
    heads = bias_table.shape[1]
    width = cache_keys.shape[1]
    trainer_rows = joined_weight.shape[0]
    hidden_units = upward_weight.shape[1] // ways
    attn_width = output_weight.shape[1]
    columns = attn_width + 2 * hidden_units
    span = bucket_index.shape[0] + 1

    joined_blocks = pl.pallas_call(
        joined_kernel,
        name="cut_joined",
        out_shape=[jax.ShapeDtypeStruct((trainer_rows, 3 * width), HALF)] * ways,
        in_specs=[HBM],
        out_specs=[VMEM] * ways,
        scratch_shapes=[
            pltpu.VMEM(joined_weight.shape, FULL),
            pltpu.SemaphoreType.DMA((1,)),
        ],
        compiler_params=params(VMEM_GRANT),
    )(joined_weight)
    forward = pl.pallas_call(
        forward_kernel,
        name="cut_forward",
        out_shape=jax.ShapeDtypeStruct((ways, trainer_rows, columns), HALF),
        in_specs=[ANY, HBM, HBM, HBM],
        out_specs=VMEM,
        scratch_shapes=[
            pltpu.VMEM(weight.shape, FULL)
            for weight in (output_weight, upward_weight, downward_weight)
        ]
        + [pltpu.SemaphoreType.DMA((3,))],
        compiler_params=params(VMEM_GRANT),
    )(joined_blocks[0], output_weight, upward_weight, downward_weight)
    own_joined, joined_blocks = joined_blocks[0], exchange(joined_blocks)

    normed, bias = pl.pallas_call(
        prepare_kernel,
        name="prepare",
        out_shape=[
            jax.ShapeDtypeStruct((rows, features), HALF),
            jax.ShapeDtypeStruct((heads, rows, cached + rows), FULL),
        ],
        in_specs=[ANY, HBM, HBM, HBM, VMEM, VMEM, VMEM, VMEM],
        out_specs=[VMEM, VMEM],
        scratch_shapes=[
            pltpu.SMEM((3,) + new_counts.shape, jnp.int32),
            pltpu.VMEM((1, span), jnp.int32),
            pltpu.SemaphoreType.DMA((3,)),
        ],
        compiler_params=params(VMEM_GRANT),
        cost_estimate=cost(10**8, 4 * 10**6),
    )(
        own_joined,
        cached_lengths,
        extend_flags,
        new_counts,
        tokens,
        first_gain.reshape(1, features),
        bias_table.T,
        bucket_index.reshape(1, span - 1),
    )

    if places == 8:
        lead = (places, ways, trainer_rows)
        forward, *joined_blocks = together(forward, *joined_blocks)
        joined = stack(joined_blocks)
        near, far, normed = together(*first_hops(joined), normed)
        held = whole_hop(joined, near, far)
        joined_pieces, joined_all = with_cores(held)
    else:
        lead = (features,)
        natural = [lax.select_n(mine ^ t, *joined_blocks) for t in range(ways)]
        joined_pieces, joined_all = [None], [natural_gather(jnp.stack(natural))]
    forward = owners_blocks(forward)

    attention = pl.pallas_call(
        functools.partial(attend_kernel, joined_pieces),
        name="attend",
        out_shape=jax.ShapeDtypeStruct((rows, width), HALF),
        in_specs=[VMEM, VMEM, VMEM, VMEM] + [ANY] * len(joined_all),
        out_specs=VMEM,
        scratch_shapes=[pltpu.VMEM(lead + (3 * width,), HALF), pltpu.SemaphoreType.DMA((8,))],
        compiler_params=params(VMEM_GRANT),
        cost_estimate=cost(ATTEND_COST, 6 * 10**6),
    )(normed, cache_keys, cache_values, bias, *joined_all)

    attended = [attention] + [swap(attention, "tensor", k) for k in range(1, ways)]
    if places == 8:
        forward_pieces, forward_all = with_cores(half_hops(forward, *first_hops(forward)))
    else:
        forward_pieces, forward_all = [None], [natural_gather(forward)]
    share = rows // ways
    own, *sends = pl.pallas_call(
        functools.partial(layer_kernel, forward_pieces, ways),
        name="layer",
        out_shape=[jax.ShapeDtypeStruct((share, features), FULL)]
        + [jax.ShapeDtypeStruct((share, features), HALF)] * (ways - 1),
        in_specs=[VMEM, VMEM] + [VMEM] * ways + [ANY] * len(forward_all),
        out_specs=[VMEM] * ways,
        scratch_shapes=[
            pltpu.VMEM(lead + (attn_width,), HALF),
            pltpu.VMEM(lead + (hidden_units,), HALF),
            pltpu.VMEM(lead + (hidden_units,), HALF),
            pltpu.VMEM((rows, attn_width), HALF),
            pltpu.VMEM((rows, features), FULL),
            pltpu.VMEM((rows, features), FULL),
            pltpu.SemaphoreType.DMA((3, len(forward_all))),
        ],
        compiler_params=params(VMEM_GRANT),
        cost_estimate=cost(2 * 10**9, 8 * 10**6),
    )(tokens, second_gain.reshape(1, features), *attended, *forward_all)

    total = own
    for k, send in enumerate(sends, 1):
        total = total + swap(send, "tensor", k).astype(FULL)
    return total.astype(HALF)


def solution(mesh):
    return jax.shard_map(
        shards,
        mesh=mesh,
        in_specs=(
            P("seq", None),
            P("seq", "tensor"),
            P("seq", "tensor"),
            P(("seq", "tensor"), None),
            P(("seq", "tensor"), None),
            P(("seq", "tensor"), None),
            P(("seq", "tensor"), None),
            P(),
            P(),
            P(None, "tensor"),
            P(),
            P(),
            P(),
            P(),
        ),
        out_specs=P(("seq", "tensor"), None),
        check_vma=False,
    )
```

```python
import functools

import jax
import jax.numpy as jnp
from jax import lax
from jax.experimental import pallas as pl
from jax.experimental.pallas import tpu as pltpu
from jax.sharding import PartitionSpec as P

EPSILON = 1e-06
FLOOR_SCORE = -1e30
HALF = jnp.bfloat16
FULL = jnp.float32
VMEM_GRANT = 32
CUT_GRANT = 60
ATTEND_COST = 2 * 10**10

VMEM = pl.BlockSpec(memory_space=pltpu.VMEM)
SMEM = pl.BlockSpec(memory_space=pltpu.SMEM)
HBM = pl.BlockSpec(memory_space=pltpu.HBM)
ANY = pl.BlockSpec(memory_space=pl.ANY)


def params(megabytes):
    return pltpu.CompilerParams(vmem_limit_bytes=megabytes * 1024 * 1024)


def cost(flops, bytes_accessed):
    return pl.CostEstimate(flops=flops, bytes_accessed=bytes_accessed, transcendentals=0)


def swap(array, axis, mask):
    size = lax.axis_size(axis)
    return lax.ppermute(array, axis, [(i, i ^ mask) for i in range(size)])


def dot(left, right):
    return jnp.dot(left, right, preferred_element_type=FULL)


def dot_nt(left, right):
    return lax.dot_general(left, right, (((1,), (1,)), ((), ())), preferred_element_type=FULL)


def here():
    return lax.axis_index("tensor"), lax.axis_index("seq")


def load(sources, targets, sems):
    copies = [
        pltpu.make_async_copy(source, target, sems.at[i])
        for i, (source, target) in enumerate(zip(sources, targets))
    ]
    for copy in copies:
        copy.start()
    for copy in copies:
        copy.wait()


def cut_kernel(*refs):
    sources, outs, (joined, output, upward, downward, sems) = refs[:4], refs[4:-5], refs[-5:]
    load(sources, [joined, output, upward, downward], sems)
    mine, _ = here()
    blocks, forward = outs[:-1], outs[-1]
    ways = len(blocks)
    part = joined.shape[1] // (3 * ways)
    for k in range(ways):
        for i in range(3):
            start = pl.multiple_of((i * ways + (mine ^ k)) * part, 128)
            blocks[k][:, i * part : (i + 1) * part] = joined[:, pl.ds(start, part)].astype(HALF)
    whole = output.shape[1]
    width = upward.shape[1] // ways
    output_half = output[...].astype(HALF)
    for t in range(ways):
        forward[t, :, :whole] = output_half
        forward[t, :, whole : whole + width] = upward[:, t * width : (t + 1) * width].astype(HALF)
        forward[t, :, whole + width :] = downward[:, t * width : (t + 1) * width].astype(HALF)


def rms_rows(rows, gain):
    mean_square = jnp.mean(rows * rows, axis=-1, keepdims=True)
    return (rows * lax.rsqrt(mean_square + EPSILON) * gain).astype(HALF)


def prepare_kernel(after, lengths, flags, counts, tokens, gain, table, buckets, normed, bias, *refs):
    numbers, padded, sems = refs
    load([lengths, flags, counts], [numbers.at[i] for i in range(3)], sems)
    _, place = here()
    used = numbers[0, place] * numbers[1, place]
    count = numbers[2, place]
    padded[...] = jnp.zeros_like(padded)
    padded[:, : buckets.shape[1]] = buckets[...]
    normed[...] = rms_rows(tokens[...].astype(FULL), gain[...])
    heads, rows, keys = bias.shape
    cached = keys - rows
    spread = padded.shape[1]
    hot = lax.broadcasted_iota(jnp.int32, (table.shape[1], spread), 0) == padded[...]
    rows_of_heads = jnp.dot(
        table[...],
        hot.astype(FULL),
        precision=lax.Precision.HIGHEST,
        preferred_element_type=FULL,
    )
    slots = lax.broadcasted_iota(jnp.int32, (rows, rows), 1)
    old_slots = lax.broadcasted_iota(jnp.int32, (rows, cached), 1)
    for h in range(heads):
        rel = jnp.broadcast_to(rows_of_heads[h : h + 1], (8, spread))
        middle = spread // 2
        old_row = pltpu.roll(rel, used + (spread - (middle - rows)), 1)[:1, : rows + cached]
        new_row = rel[:1, middle - rows : middle + rows]
        old = jnp.broadcast_to(old_row, (rows, rows + cached))
        old = pltpu.roll(old, cached + 1, 1, stride=1, stride_axis=0)[:, :cached]
        new = jnp.broadcast_to(new_row, (rows, 2 * rows))
        new = pltpu.roll(new, rows + 1, 1, stride=1, stride_axis=0)[:, :rows]
        bias[h, :, :cached] = jnp.where(old_slots < used, old, FLOOR_SCORE)
        bias[h, :, cached:] = jnp.where(slots < count, new, FLOOR_SCORE)


def stack_kernel(ways, *refs):
    target, sems = refs[-2:]
    mine, _ = here()
    load(refs[:ways], [target.at[mine ^ k] for k in range(ways)], sems)


def stack(blocks, *after):
    ways = len(blocks)
    return pl.pallas_call(
        functools.partial(stack_kernel, ways),
        name="stack",
        out_shape=jax.ShapeDtypeStruct((ways,) + blocks[0].shape, HALF),
        in_specs=[HBM] * ways + [ANY] * len(after),
        out_specs=VMEM,
        scratch_shapes=[pltpu.SemaphoreType.DMA((ways,))],
        compiler_params=params(VMEM_GRANT),
    )(*blocks, *after)


def gather_copies(pieces, sources, start, target, sems):
    width = target.shape[-1]
    if len(sources) == 1:
        source = sources[0].at[:, start : start + width]
        return [pltpu.make_async_copy(source, target, sems.at[0])]
    _, place = here()
    copies = []
    for i, ((j, t), source) in enumerate(zip(pieces, sources)):
        block = target.at[place ^ j, t : t + source.shape[0]]
        source = source.at[:, :, start : start + width]
        copies.append(pltpu.make_async_copy(source, block, sems.at[i]))
    return copies


def attend_kernel(pieces, normed, old_keys, old_values, bias, *refs):
    sources, (out, weight, sems) = refs[: len(pieces)], refs[len(pieces) :]
    copies = gather_copies(pieces, sources, 0, weight, sems)
    for copy in copies:
        copy.start()
    for copy in copies:
        copy.wait()
    rows, features = normed.shape
    heads = bias.shape[0]
    width = out.shape[1]
    size = width // heads
    projected = dot(normed[...], weight[...].reshape(features, 3 * width)).astype(HALF)
    queries = projected[:, :width]
    new_keys = projected[:, width : 2 * width]
    new_values = projected[:, 2 * width :]
    cached = old_keys.shape[0]
    lanes = lax.broadcasted_iota(jnp.int32, (rows, width), 1)
    result = jnp.zeros((rows, width), FULL)
    for h in range(heads):
        inside = (lanes >= h * size) & (lanes < (h + 1) * size)
        query = jnp.where(inside, queries, jnp.zeros_like(queries))
        old = dot_nt(query, old_keys[...]) + bias[h, :, :cached]
        new = dot_nt(query, new_keys) + bias[h, :, cached:]
        top = jnp.maximum(
            jnp.max(old, axis=1, keepdims=True), jnp.max(new, axis=1, keepdims=True)
        )
        old = jnp.exp(old - top)
        new = jnp.exp(new - top)
        total = jnp.sum(old, axis=1, keepdims=True) + jnp.sum(new, axis=1, keepdims=True)
        mixed = dot(old.astype(HALF), old_values[...]) + dot(new.astype(HALF), new_values)
        result = jnp.where(inside, mixed / total, result)
    out[...] = result.astype(HALF)


def layer_kernel(pieces, ways, tokens, gain, *refs):
    attended, refs = refs[:ways], refs[ways:]
    sources, refs = refs[: len(pieces)], refs[len(pieces) :]
    outs, (output, upward, downward, attention, hidden, feed, sems) = refs[:ways], refs[ways:]
    features = tokens.shape[1]
    copies, start = [], 0
    for i, weight in enumerate((output, upward, downward)):
        copies.append(gather_copies(pieces, sources, start, weight, sems.at[i]))
        start += weight.shape[-1]
        for copy in copies[-1]:
            copy.start()
    mine, _ = here()
    width = attended[0].shape[1]
    for k in range(ways):
        attention[:, pl.ds(pl.multiple_of((mine ^ k) * width, 128), width)] = attended[k][...]

    def arrived(i, weight):
        for copy in copies[i]:
            copy.wait()
        return weight[...].reshape(features, -1)

    hidden[...] = tokens[...].astype(FULL) + dot_nt(attention[...], arrived(0, output))
    inner = dot(rms_rows(hidden[...], gain[...]), arrived(1, upward))
    active = jnp.maximum(inner, 0.0).astype(HALF)
    feed[...] = dot_nt(active, arrived(2, downward))
    share = tokens.shape[0] // ways
    for k in range(ways):
        rows_of = pl.ds(pl.multiple_of((mine ^ k) * share, 8), share)
        if k == 0:
            outs[0][...] = hidden[rows_of, :] + feed[rows_of, :]
        else:
            outs[k][...] = feed[rows_of, :].astype(HALF)


def exchange(blocks):
    return [blocks[0]] + [swap(block, "tensor", k) for k, block in enumerate(blocks) if k]


def natural_gather(rows):
    return lax.all_gather(rows.reshape(-1, rows.shape[-1]), "seq", axis=0, tiled=True)


def together(*arrays):
    return lax.optimization_barrier(arrays)


NEAR, FAR = 4, 2


def first_hops(block):
    return together(swap(block, "seq", NEAR), swap(block, "seq", FAR))


def with_cores(held):
    for (j, t), piece in list(held.items()):
        held[j | 1, t] = swap(piece, "seq", 1)
    return list(held), list(held.values())


def whole_hop(block, near, far):
    held = {(0, 0): block, (NEAR, 0): near, (FAR, 0): far}
    held[NEAR | FAR, 0] = swap(near, "seq", FAR)
    return held


def half_hops(block, near, far):
    half = block.shape[0] // 2
    held = {(0, 0): block, (NEAR, 0): near, (FAR, 0): far}
    held[NEAR | FAR, 0] = swap(near[:half], "seq", FAR)
    held[NEAR | FAR, half] = swap(far[half:], "seq", NEAR)
    return held


def owners_blocks(blocks):
    return lax.all_to_all(blocks, "tensor", split_axis=0, concat_axis=0, tiled=True)


def shards(
    tokens,
    cache_keys,
    cache_values,
    joined_weight,
    output_weight,
    upward_weight,
    downward_weight,
    first_gain,
    second_gain,
    bias_table,
    bucket_index,
    cached_lengths,
    new_counts,
    extend_flags,
):
    ways = lax.axis_size("tensor")
    places = lax.axis_size("seq")
    mine = lax.axis_index("tensor")
    rows, features = tokens.shape
    cached = cache_keys.shape[0]
    heads = bias_table.shape[1]
    width = cache_keys.shape[1]
    trainer_rows = joined_weight.shape[0]
    hidden_units = upward_weight.shape[1] // ways
    attn_width = output_weight.shape[1]
    columns = attn_width + 2 * hidden_units
    span = bucket_index.shape[0] + 1

    weights = (joined_weight, output_weight, upward_weight, downward_weight)
    *joined_blocks, forward = pl.pallas_call(
        cut_kernel,
        name="cut",
        out_shape=[jax.ShapeDtypeStruct((trainer_rows, 3 * width), HALF)] * ways
        + [jax.ShapeDtypeStruct((ways, trainer_rows, columns), HALF)],
        in_specs=[HBM] * 4,
        out_specs=[VMEM] * (1 + ways),
        scratch_shapes=[pltpu.VMEM(weight.shape, FULL) for weight in weights]
        + [pltpu.SemaphoreType.DMA((4,))],
        compiler_params=params(CUT_GRANT),
    )(*weights)
    own_joined, joined_blocks = joined_blocks[0], exchange(joined_blocks)

    normed, bias = pl.pallas_call(
        prepare_kernel,
        name="prepare",
        out_shape=[
            jax.ShapeDtypeStruct((rows, features), HALF),
            jax.ShapeDtypeStruct((heads, rows, cached + rows), FULL),
        ],
        in_specs=[ANY, HBM, HBM, HBM, VMEM, VMEM, VMEM, VMEM],
        out_specs=[VMEM, VMEM],
        scratch_shapes=[
            pltpu.SMEM((3,) + new_counts.shape, jnp.int32),
            pltpu.VMEM((1, span), jnp.int32),
            pltpu.SemaphoreType.DMA((3,)),
        ],
        compiler_params=params(VMEM_GRANT),
        cost_estimate=cost(2 * 10**10, 4 * 10**6),
    )(
        own_joined,
        cached_lengths,
        extend_flags,
        new_counts,
        tokens,
        first_gain.reshape(1, features),
        bias_table.T,
        bucket_index.reshape(1, span - 1),
    )

    if places == 8:
        lead = (places, ways, trainer_rows)
        joined = stack(joined_blocks, normed)
        near, far = first_hops(joined)
        held = whole_hop(joined, near, far)
        joined_pieces, joined_all = with_cores(held)
    else:
        lead = (features,)
        natural = [lax.select_n(mine ^ t, *joined_blocks) for t in range(ways)]
        joined_pieces, joined_all = [None], [natural_gather(jnp.stack(natural))]
    forward = owners_blocks(forward)

    attention = pl.pallas_call(
        functools.partial(attend_kernel, joined_pieces),
        name="attend",
        out_shape=jax.ShapeDtypeStruct((rows, width), HALF),
        in_specs=[VMEM, VMEM, VMEM, VMEM] + [ANY] * len(joined_all),
        out_specs=VMEM,
        scratch_shapes=[pltpu.VMEM(lead + (3 * width,), HALF), pltpu.SemaphoreType.DMA((8,))],
        compiler_params=params(VMEM_GRANT),
        cost_estimate=cost(ATTEND_COST, 6 * 10**6),
    )(normed, cache_keys, cache_values, bias, *joined_all)

    attended = [attention] + [swap(attention, "tensor", k) for k in range(1, ways)]
    if places == 8:
        forward_pieces, forward_all = with_cores(half_hops(forward, *first_hops(forward)))
    else:
        forward_pieces, forward_all = [None], [natural_gather(forward)]
    share = rows // ways
    own, *sends = pl.pallas_call(
        functools.partial(layer_kernel, forward_pieces, ways),
        name="layer",
        out_shape=[jax.ShapeDtypeStruct((share, features), FULL)]
        + [jax.ShapeDtypeStruct((share, features), HALF)] * (ways - 1),
        in_specs=[VMEM, VMEM] + [VMEM] * ways + [ANY] * len(forward_all),
        out_specs=[VMEM] * ways,
        scratch_shapes=[
            pltpu.VMEM(lead + (attn_width,), HALF),
            pltpu.VMEM(lead + (hidden_units,), HALF),
            pltpu.VMEM(lead + (hidden_units,), HALF),
            pltpu.VMEM((rows, attn_width), HALF),
            pltpu.VMEM((rows, features), FULL),
            pltpu.VMEM((rows, features), FULL),
            pltpu.SemaphoreType.DMA((3, len(forward_all))),
        ],
        compiler_params=params(VMEM_GRANT),
        cost_estimate=cost(2 * 10**9, 8 * 10**6),
    )(tokens, second_gain.reshape(1, features), *attended, *forward_all)

    total = own
    for k, send in enumerate(sends, 1):
        total = total + swap(send, "tensor", k).astype(FULL)
    return total.astype(HALF)


def solution(mesh):
    return jax.shard_map(
        shards,
        mesh=mesh,
        in_specs=(
            P("seq", None),
            P("seq", "tensor"),
            P("seq", "tensor"),
            P(("seq", "tensor"), None),
            P(("seq", "tensor"), None),
            P(("seq", "tensor"), None),
            P(("seq", "tensor"), None),
            P(),
            P(),
            P(None, "tensor"),
            P(),
            P(),
            P(),
            P(),
        ),
        out_specs=P(("seq", "tensor"), None),
        check_vma=False,
    )
```

```python
import functools

import jax
import jax.numpy as jnp
from jax import lax
from jax.experimental import pallas as pl
from jax.experimental.pallas import tpu as pltpu
from jax.sharding import PartitionSpec as P

EPSILON = 1e-06
FLOOR_SCORE = -1e30
HALF = jnp.bfloat16
FULL = jnp.float32
VMEM_GRANT = 32
CUT_GRANT = 60
ATTEND_COST = 2 * 10**10

VMEM = pl.BlockSpec(memory_space=pltpu.VMEM)
SMEM = pl.BlockSpec(memory_space=pltpu.SMEM)
HBM = pl.BlockSpec(memory_space=pltpu.HBM)
ANY = pl.BlockSpec(memory_space=pl.ANY)


def params(megabytes):
    return pltpu.CompilerParams(vmem_limit_bytes=megabytes * 1024 * 1024)


def cost(flops, bytes_accessed):
    return pl.CostEstimate(flops=flops, bytes_accessed=bytes_accessed, transcendentals=0)


def swap(array, axis, mask):
    size = lax.axis_size(axis)
    return lax.ppermute(array, axis, [(i, i ^ mask) for i in range(size)])


def dot(left, right):
    return jnp.dot(left, right, preferred_element_type=FULL)


def dot_nt(left, right):
    return lax.dot_general(left, right, (((1,), (1,)), ((), ())), preferred_element_type=FULL)


def here():
    return lax.axis_index("tensor"), lax.axis_index("seq")


def load(sources, targets, sems):
    copies = [
        pltpu.make_async_copy(source, target, sems.at[i])
        for i, (source, target) in enumerate(zip(sources, targets))
    ]
    for copy in copies:
        copy.start()
    for copy in copies:
        copy.wait()


def cut_kernel(*refs):
    sources, outs, (joined, output, upward, downward, sems) = refs[:4], refs[4:-5], refs[-5:]
    load(sources, [joined, output, upward, downward], sems)
    mine, _ = here()
    blocks, forward = outs[:-1], outs[-1]
    ways = len(blocks)
    part = joined.shape[1] // (3 * ways)
    for k in range(ways):
        for i in range(3):
            start = pl.multiple_of((i * ways + (mine ^ k)) * part, 128)
            blocks[k][:, i * part : (i + 1) * part] = joined[:, pl.ds(start, part)].astype(HALF)
    whole = output.shape[1]
    width = upward.shape[1] // ways
    output_half = output[...].astype(HALF)
    for t in range(ways):
        forward[t, :, :whole] = output_half
        forward[t, :, whole : whole + width] = upward[:, t * width : (t + 1) * width].astype(HALF)
        forward[t, :, whole + width :] = downward[:, t * width : (t + 1) * width].astype(HALF)


def rms_rows(rows, gain):
    mean_square = jnp.mean(rows * rows, axis=-1, keepdims=True)
    return (rows * lax.rsqrt(mean_square + EPSILON) * gain).astype(HALF)


def prepare_kernel(after, lengths, flags, counts, tokens, gain, table, buckets, normed, bias, *refs):
    numbers, padded, sems = refs
    load([lengths, flags, counts], [numbers.at[i] for i in range(3)], sems)
    _, place = here()
    used = numbers[0, place] * numbers[1, place]
    count = numbers[2, place]
    padded[...] = jnp.zeros_like(padded)
    padded[:, : buckets.shape[1]] = buckets[...]
    normed[...] = rms_rows(tokens[...].astype(FULL), gain[...])
    heads, rows, keys = bias.shape
    cached = keys - rows
    spread = padded.shape[1]
    hot = lax.broadcasted_iota(jnp.int32, (table.shape[1], spread), 0) == padded[...]
    rows_of_heads = jnp.dot(
        table[...],
        hot.astype(FULL),
        precision=lax.Precision.HIGHEST,
        preferred_element_type=FULL,
    )
    slots = lax.broadcasted_iota(jnp.int32, (rows, rows), 1)
    old_slots = lax.broadcasted_iota(jnp.int32, (rows, cached), 1)
    for h in range(heads):
        rel = jnp.broadcast_to(rows_of_heads[h : h + 1], (8, spread))
        middle = spread // 2
        old_row = pltpu.roll(rel, used + (spread - (middle - rows)), 1)[:1, : rows + cached]
        new_row = rel[:1, middle - rows : middle + rows]
        old = jnp.broadcast_to(old_row, (rows, rows + cached))
        old = pltpu.roll(old, cached + 1, 1, stride=1, stride_axis=0)[:, :cached]
        new = jnp.broadcast_to(new_row, (rows, 2 * rows))
        new = pltpu.roll(new, rows + 1, 1, stride=1, stride_axis=0)[:, :rows]
        bias[h, :, :cached] = jnp.where(old_slots < used, old, FLOOR_SCORE)
        bias[h, :, cached:] = jnp.where(slots < count, new, FLOOR_SCORE)


def stack_kernel(ways, *refs):
    target, sems = refs[-2:]
    mine, _ = here()
    load(refs[:ways], [target.at[mine ^ k] for k in range(ways)], sems)


def stack(blocks, *after):
    ways = len(blocks)
    return pl.pallas_call(
        functools.partial(stack_kernel, ways),
        name="stack",
        out_shape=jax.ShapeDtypeStruct((ways,) + blocks[0].shape, HALF),
        in_specs=[HBM] * ways + [ANY] * len(after),
        out_specs=VMEM,
        scratch_shapes=[pltpu.SemaphoreType.DMA((ways,))],
        compiler_params=params(VMEM_GRANT),
    )(*blocks, *after)


def gather_copies(pieces, sources, start, target, sems):
    width = target.shape[-1]
    if len(sources) == 1:
        source = sources[0].at[:, start : start + width]
        return [pltpu.make_async_copy(source, target, sems.at[0])]
    _, place = here()
    copies = []
    for i, ((j, t), source) in enumerate(zip(pieces, sources)):
        block = target.at[place ^ j, t : t + source.shape[0]]
        source = source.at[:, :, start : start + width]
        copies.append(pltpu.make_async_copy(source, block, sems.at[i]))
    return copies


def attend_kernel(pieces, normed, old_keys, old_values, bias, *refs):
    sources, (out, weight, sems) = refs[: len(pieces)], refs[len(pieces) :]
    copies = gather_copies(pieces, sources, 0, weight, sems)
    for copy in copies:
        copy.start()
    for copy in copies:
        copy.wait()
    rows, features = normed.shape
    heads = bias.shape[0]
    width = out.shape[1]
    size = width // heads
    projected = dot(normed[...], weight[...].reshape(features, 3 * width)).astype(HALF)
    queries = projected[:, :width]
    new_keys = projected[:, width : 2 * width]
    new_values = projected[:, 2 * width :]
    cached = old_keys.shape[0]
    lanes = lax.broadcasted_iota(jnp.int32, (rows, width), 1)
    result = jnp.zeros((rows, width), FULL)
    for h in range(heads):
        inside = (lanes >= h * size) & (lanes < (h + 1) * size)
        query = jnp.where(inside, queries, jnp.zeros_like(queries))
        old = dot_nt(query, old_keys[...]) + bias[h, :, :cached]
        new = dot_nt(query, new_keys) + bias[h, :, cached:]
        top = jnp.maximum(
            jnp.max(old, axis=1, keepdims=True), jnp.max(new, axis=1, keepdims=True)
        )
        old = jnp.exp(old - top)
        new = jnp.exp(new - top)
        total = jnp.sum(old, axis=1, keepdims=True) + jnp.sum(new, axis=1, keepdims=True)
        mixed = dot(old.astype(HALF), old_values[...]) + dot(new.astype(HALF), new_values)
        result = jnp.where(inside, mixed / total, result)
    out[...] = result.astype(HALF)


def layer_kernel(pieces, ways, tokens, gain, *refs):
    attended, refs = refs[:ways], refs[ways:]
    sources, refs = refs[: len(pieces)], refs[len(pieces) :]
    outs, (output, upward, downward, attention, hidden, feed, sems) = refs[:ways], refs[ways:]
    features = tokens.shape[1]
    copies, start = [], 0
    for i, weight in enumerate((output, upward, downward)):
        copies.append(gather_copies(pieces, sources, start, weight, sems.at[i]))
        start += weight.shape[-1]
        for copy in copies[-1]:
            copy.start()
    mine, _ = here()
    width = attended[0].shape[1]
    for k in range(ways):
        attention[:, pl.ds(pl.multiple_of((mine ^ k) * width, 128), width)] = attended[k][...]

    def arrived(i, weight):
        for copy in copies[i]:
            copy.wait()
        return weight[...].reshape(features, -1)

    hidden[...] = tokens[...].astype(FULL) + dot_nt(attention[...], arrived(0, output))
    inner = dot(rms_rows(hidden[...], gain[...]), arrived(1, upward))
    active = jnp.maximum(inner, 0.0).astype(HALF)
    feed[...] = dot_nt(active, arrived(2, downward))
    share = tokens.shape[0] // ways
    for k in range(ways):
        rows_of = pl.ds(pl.multiple_of((mine ^ k) * share, 8), share)
        if k == 0:
            outs[0][...] = hidden[rows_of, :] + feed[rows_of, :]
        else:
            outs[k][...] = feed[rows_of, :].astype(HALF)


def exchange(blocks):
    return [blocks[0]] + [swap(block, "tensor", k) for k, block in enumerate(blocks) if k]


def natural_gather(rows):
    return lax.all_gather(rows.reshape(-1, rows.shape[-1]), "seq", axis=0, tiled=True)


def together(*arrays):
    return lax.optimization_barrier(arrays)


NEAR, FAR = 4, 2


def first_hops(block):
    return together(swap(block, "seq", NEAR), swap(block, "seq", FAR))


def with_cores(held):
    for (j, t), piece in list(held.items()):
        held[j | 1, t] = swap(piece, "seq", 1)
    return list(held), list(held.values())


def whole_hop(block, near, far):
    held = {(0, 0): block, (NEAR, 0): near, (FAR, 0): far}
    held[NEAR | FAR, 0] = swap(near, "seq", FAR)
    return held


def half_hops(block, near, far):
    half = block.shape[0] // 2
    held = {(0, 0): block, (NEAR, 0): near, (FAR, 0): far}
    held[NEAR | FAR, 0] = swap(near[:half], "seq", FAR)
    held[NEAR | FAR, half] = swap(far[half:], "seq", NEAR)
    return held


def owners_blocks(blocks):
    return lax.all_to_all(blocks, "tensor", split_axis=0, concat_axis=0, tiled=True)


def shards(
    tokens,
    cache_keys,
    cache_values,
    joined_weight,
    output_weight,
    upward_weight,
    downward_weight,
    first_gain,
    second_gain,
    bias_table,
    bucket_index,
    cached_lengths,
    new_counts,
    extend_flags,
):
    ways = lax.axis_size("tensor")
    places = lax.axis_size("seq")
    mine = lax.axis_index("tensor")
    rows, features = tokens.shape
    cached = cache_keys.shape[0]
    heads = bias_table.shape[1]
    width = cache_keys.shape[1]
    trainer_rows = joined_weight.shape[0]
    hidden_units = upward_weight.shape[1] // ways
    attn_width = output_weight.shape[1]
    columns = attn_width + 2 * hidden_units
    span = bucket_index.shape[0] + 1

    weights = (joined_weight, output_weight, upward_weight, downward_weight)
    *joined_blocks, forward = pl.pallas_call(
        cut_kernel,
        name="cut",
        out_shape=[jax.ShapeDtypeStruct((trainer_rows, 3 * width), HALF)] * ways
        + [jax.ShapeDtypeStruct((ways, trainer_rows, columns), HALF)],
        in_specs=[HBM] * 4,
        out_specs=[VMEM] * (1 + ways),
        scratch_shapes=[pltpu.VMEM(weight.shape, FULL) for weight in weights]
        + [pltpu.SemaphoreType.DMA((4,))],
        compiler_params=params(CUT_GRANT),
    )(*weights)
    own_joined, joined_blocks = joined_blocks[0], exchange(joined_blocks)

    normed, bias = pl.pallas_call(
        prepare_kernel,
        name="prepare",
        out_shape=[
            jax.ShapeDtypeStruct((rows, features), HALF),
            jax.ShapeDtypeStruct((heads, rows, cached + rows), FULL),
        ],
        in_specs=[ANY, HBM, HBM, HBM, VMEM, VMEM, VMEM, VMEM],
        out_specs=[VMEM, VMEM],
        scratch_shapes=[
            pltpu.SMEM((3,) + new_counts.shape, jnp.int32),
            pltpu.VMEM((1, span), jnp.int32),
            pltpu.SemaphoreType.DMA((3,)),
        ],
        compiler_params=params(VMEM_GRANT),
        cost_estimate=cost(2 * 10**10, 4 * 10**6),
    )(
        own_joined,
        cached_lengths,
        extend_flags,
        new_counts,
        tokens,
        first_gain.reshape(1, features),
        bias_table.T,
        bucket_index.reshape(1, span - 1),
    )

    if places == 8:
        lead = (places, ways, trainer_rows)
        joined = stack(joined_blocks)
        near, far, normed = together(*first_hops(joined), normed)
        held = whole_hop(joined, near, far)
        joined_pieces, joined_all = with_cores(held)
    else:
        lead = (features,)
        natural = [lax.select_n(mine ^ t, *joined_blocks) for t in range(ways)]
        joined_pieces, joined_all = [None], [natural_gather(jnp.stack(natural))]
    forward = owners_blocks(forward)

    attention = pl.pallas_call(
        functools.partial(attend_kernel, joined_pieces),
        name="attend",
        out_shape=jax.ShapeDtypeStruct((rows, width), HALF),
        in_specs=[VMEM, VMEM, VMEM, VMEM] + [ANY] * len(joined_all),
        out_specs=VMEM,
        scratch_shapes=[pltpu.VMEM(lead + (3 * width,), HALF), pltpu.SemaphoreType.DMA((8,))],
        compiler_params=params(VMEM_GRANT),
        cost_estimate=cost(ATTEND_COST, 6 * 10**6),
    )(normed, cache_keys, cache_values, bias, *joined_all)

    attended = [attention] + [swap(attention, "tensor", k) for k in range(1, ways)]
    if places == 8:
        forward_pieces, forward_all = with_cores(half_hops(forward, *first_hops(forward)))
    else:
        forward_pieces, forward_all = [None], [natural_gather(forward)]
    share = rows // ways
    own, *sends = pl.pallas_call(
        functools.partial(layer_kernel, forward_pieces, ways),
        name="layer",
        out_shape=[jax.ShapeDtypeStruct((share, features), FULL)]
        + [jax.ShapeDtypeStruct((share, features), HALF)] * (ways - 1),
        in_specs=[VMEM, VMEM] + [VMEM] * ways + [ANY] * len(forward_all),
        out_specs=[VMEM] * ways,
        scratch_shapes=[
            pltpu.VMEM(lead + (attn_width,), HALF),
            pltpu.VMEM(lead + (hidden_units,), HALF),
            pltpu.VMEM(lead + (hidden_units,), HALF),
            pltpu.VMEM((rows, attn_width), HALF),
            pltpu.VMEM((rows, features), FULL),
            pltpu.VMEM((rows, features), FULL),
            pltpu.SemaphoreType.DMA((3, len(forward_all))),
        ],
        compiler_params=params(VMEM_GRANT),
        cost_estimate=cost(2 * 10**9, 8 * 10**6),
    )(tokens, second_gain.reshape(1, features), *attended, *forward_all)

    total = own
    for k, send in enumerate(sends, 1):
        total = total + swap(send, "tensor", k).astype(FULL)
    return total.astype(HALF)


def solution(mesh):
    return jax.shard_map(
        shards,
        mesh=mesh,
        in_specs=(
            P("seq", None),
            P("seq", "tensor"),
            P("seq", "tensor"),
            P(("seq", "tensor"), None),
            P(("seq", "tensor"), None),
            P(("seq", "tensor"), None),
            P(("seq", "tensor"), None),
            P(),
            P(),
            P(None, "tensor"),
            P(),
            P(),
            P(),
            P(),
        ),
        out_specs=P(("seq", "tensor"), None),
        check_vma=False,
    )
```

```python
import functools

import jax
import jax.numpy as jnp
from jax import lax
from jax.experimental import pallas as pl
from jax.experimental.pallas import tpu as pltpu
from jax.sharding import PartitionSpec as P

EPSILON = 1e-06
FLOOR_SCORE = -1e30
HALF = jnp.bfloat16
FULL = jnp.float32
VMEM_GRANT = 32
CUT_GRANT = 60
ATTEND_COST = 2 * 10**10

VMEM = pl.BlockSpec(memory_space=pltpu.VMEM)
SMEM = pl.BlockSpec(memory_space=pltpu.SMEM)
HBM = pl.BlockSpec(memory_space=pltpu.HBM)
ANY = pl.BlockSpec(memory_space=pl.ANY)


def params(megabytes):
    return pltpu.CompilerParams(vmem_limit_bytes=megabytes * 1024 * 1024)


def cost(flops, bytes_accessed):
    return pl.CostEstimate(flops=flops, bytes_accessed=bytes_accessed, transcendentals=0)


def swap(array, axis, mask):
    size = lax.axis_size(axis)
    return lax.ppermute(array, axis, [(i, i ^ mask) for i in range(size)])


def dot(left, right):
    return jnp.dot(left, right, preferred_element_type=FULL)


def dot_nt(left, right):
    return lax.dot_general(left, right, (((1,), (1,)), ((), ())), preferred_element_type=FULL)


def here():
    return lax.axis_index("tensor"), lax.axis_index("seq")


def load(sources, targets, sems):
    copies = [
        pltpu.make_async_copy(source, target, sems.at[i])
        for i, (source, target) in enumerate(zip(sources, targets))
    ]
    for copy in copies:
        copy.start()
    for copy in copies:
        copy.wait()


def cut_kernel(*refs):
    sources, outs, (joined, output, upward, downward, sems) = refs[:4], refs[4:-5], refs[-5:]
    load(sources, [joined, output, upward, downward], sems)
    mine, _ = here()
    blocks, forward = outs[:-1], outs[-1]
    ways = len(blocks)
    part = joined.shape[1] // (3 * ways)
    for k in range(ways):
        for i in range(3):
            start = pl.multiple_of((i * ways + (mine ^ k)) * part, 128)
            blocks[k][:, i * part : (i + 1) * part] = joined[:, pl.ds(start, part)].astype(HALF)
    whole = output.shape[1]
    width = upward.shape[1] // ways
    output_half = output[...].astype(HALF)
    for t in range(ways):
        forward[t, :, :whole] = output_half
        forward[t, :, whole : whole + width] = upward[:, t * width : (t + 1) * width].astype(HALF)
        forward[t, :, whole + width :] = downward[:, t * width : (t + 1) * width].astype(HALF)


def rms_rows(rows, gain):
    mean_square = jnp.mean(rows * rows, axis=-1, keepdims=True)
    return (rows * lax.rsqrt(mean_square + EPSILON) * gain).astype(HALF)


def prepare_kernel(after, lengths, flags, counts, tokens, gain, table, buckets, normed, bias, *refs):
    numbers, padded, sems = refs
    load([lengths, flags, counts], [numbers.at[i] for i in range(3)], sems)
    _, place = here()
    used = numbers[0, place] * numbers[1, place]
    count = numbers[2, place]
    padded[...] = jnp.zeros_like(padded)
    padded[:, : buckets.shape[1]] = buckets[...]
    normed[...] = rms_rows(tokens[...].astype(FULL), gain[...])
    heads, rows, keys = bias.shape
    cached = keys - rows
    spread = padded.shape[1]
    hot = lax.broadcasted_iota(jnp.int32, (table.shape[1], spread), 0) == padded[...]
    rows_of_heads = jnp.dot(
        table[...],
        hot.astype(FULL),
        precision=lax.Precision.HIGHEST,
        preferred_element_type=FULL,
    )
    slots = lax.broadcasted_iota(jnp.int32, (rows, rows), 1)
    old_slots = lax.broadcasted_iota(jnp.int32, (rows, cached), 1)
    for h in range(heads):
        rel = jnp.broadcast_to(rows_of_heads[h : h + 1], (8, spread))
        middle = spread // 2
        old_row = pltpu.roll(rel, used + (spread - (middle - rows)), 1)[:1, : rows + cached]
        new_row = rel[:1, middle - rows : middle + rows]
        old = jnp.broadcast_to(old_row, (rows, rows + cached))
        old = pltpu.roll(old, cached + 1, 1, stride=1, stride_axis=0)[:, :cached]
        new = jnp.broadcast_to(new_row, (rows, 2 * rows))
        new = pltpu.roll(new, rows + 1, 1, stride=1, stride_axis=0)[:, :rows]
        bias[h, :, :cached] = jnp.where(old_slots < used, old, FLOOR_SCORE)
        bias[h, :, cached:] = jnp.where(slots < count, new, FLOOR_SCORE)


def stack_kernel(ways, *refs):
    target, sems = refs[-2:]
    mine, _ = here()
    load(refs[:ways], [target.at[mine ^ k] for k in range(ways)], sems)


def stack(blocks, *after):
    ways = len(blocks)
    return pl.pallas_call(
        functools.partial(stack_kernel, ways),
        name="stack",
        out_shape=jax.ShapeDtypeStruct((ways,) + blocks[0].shape, HALF),
        in_specs=[HBM] * ways + [ANY] * len(after),
        out_specs=VMEM,
        scratch_shapes=[pltpu.SemaphoreType.DMA((ways,))],
        compiler_params=params(VMEM_GRANT),
    )(*blocks, *after)


def gather_copies(pieces, sources, start, target, sems):
    width = target.shape[-1]
    if len(sources) == 1:
        source = sources[0].at[:, start : start + width]
        return [pltpu.make_async_copy(source, target, sems.at[0])]
    _, place = here()
    copies = []
    for i, ((j, t), source) in enumerate(zip(pieces, sources)):
        block = target.at[place ^ j, t : t + source.shape[0]]
        source = source.at[:, :, start : start + width]
        copies.append(pltpu.make_async_copy(source, block, sems.at[i]))
    return copies


def attend_kernel(pieces, normed, old_keys, old_values, bias, *refs):
    sources, (out, weight, sems) = refs[: len(pieces)], refs[len(pieces) :]
    copies = gather_copies(pieces, sources, 0, weight, sems)
    for copy in copies:
        copy.start()
    for copy in copies:
        copy.wait()
    rows, features = normed.shape
    heads = bias.shape[0]
    width = out.shape[1]
    size = width // heads
    projected = dot(normed[...], weight[...].reshape(features, 3 * width)).astype(HALF)
    queries = projected[:, :width]
    new_keys = projected[:, width : 2 * width]
    new_values = projected[:, 2 * width :]
    cached = old_keys.shape[0]
    lanes = lax.broadcasted_iota(jnp.int32, (rows, width), 1)
    result = jnp.zeros((rows, width), FULL)
    for h in range(heads):
        inside = (lanes >= h * size) & (lanes < (h + 1) * size)
        query = jnp.where(inside, queries, jnp.zeros_like(queries))
        old = dot_nt(query, old_keys[...]) + bias[h, :, :cached]
        new = dot_nt(query, new_keys) + bias[h, :, cached:]
        top = jnp.maximum(
            jnp.max(old, axis=1, keepdims=True), jnp.max(new, axis=1, keepdims=True)
        )
        old = jnp.exp(old - top)
        new = jnp.exp(new - top)
        total = jnp.sum(old, axis=1, keepdims=True) + jnp.sum(new, axis=1, keepdims=True)
        mixed = dot(old.astype(HALF), old_values[...]) + dot(new.astype(HALF), new_values)
        result = jnp.where(inside, mixed / total, result)
    out[...] = result.astype(HALF)


def layer_kernel(pieces, ways, tokens, gain, *refs):
    attended, refs = refs[:ways], refs[ways:]
    sources, refs = refs[: len(pieces)], refs[len(pieces) :]
    outs, (output, upward, downward, attention, hidden, feed, sems) = refs[:ways], refs[ways:]
    features = tokens.shape[1]
    copies, start = [], 0
    for i, weight in enumerate((output, upward, downward)):
        copies.append(gather_copies(pieces, sources, start, weight, sems.at[i]))
        start += weight.shape[-1]
        for copy in copies[-1]:
            copy.start()
    mine, _ = here()
    width = attended[0].shape[1]
    for k in range(ways):
        attention[:, pl.ds(pl.multiple_of((mine ^ k) * width, 128), width)] = attended[k][...]

    def arrived(i, weight):
        for copy in copies[i]:
            copy.wait()
        return weight[...].reshape(features, -1)

    hidden[...] = tokens[...].astype(FULL) + dot_nt(attention[...], arrived(0, output))
    inner = dot(rms_rows(hidden[...], gain[...]), arrived(1, upward))
    active = jnp.maximum(inner, 0.0).astype(HALF)
    feed[...] = dot_nt(active, arrived(2, downward))
    share = tokens.shape[0] // ways
    for k in range(ways):
        rows_of = pl.ds(pl.multiple_of((mine ^ k) * share, 8), share)
        if k == 0:
            outs[0][...] = hidden[rows_of, :] + feed[rows_of, :]
        else:
            outs[k][...] = feed[rows_of, :].astype(HALF)


def exchange(blocks):
    return [blocks[0]] + [swap(block, "tensor", k) for k, block in enumerate(blocks) if k]


def natural_gather(rows):
    return lax.all_gather(rows.reshape(-1, rows.shape[-1]), "seq", axis=0, tiled=True)


def together(*arrays):
    return lax.optimization_barrier(arrays)


NEAR, FAR = 4, 2


def first_hops(block):
    return together(swap(block, "seq", NEAR), swap(block, "seq", FAR))


def with_cores(held):
    for (j, t), piece in list(held.items()):
        held[j | 1, t] = swap(piece, "seq", 1)
    return list(held), list(held.values())


def whole_hop(block, near, far):
    held = {(0, 0): block, (NEAR, 0): near, (FAR, 0): far}
    held[NEAR | FAR, 0] = swap(near, "seq", FAR)
    return held


def half_hops(block, near, far):
    half = block.shape[0] // 2
    held = {(0, 0): block, (NEAR, 0): near, (FAR, 0): far}
    held[NEAR | FAR, 0] = swap(near[:half], "seq", FAR)
    held[NEAR | FAR, half] = swap(far[half:], "seq", NEAR)
    return held


def owners_blocks(blocks):
    return lax.all_to_all(blocks, "tensor", split_axis=0, concat_axis=0, tiled=True)


def shards(
    tokens,
    cache_keys,
    cache_values,
    joined_weight,
    output_weight,
    upward_weight,
    downward_weight,
    first_gain,
    second_gain,
    bias_table,
    bucket_index,
    cached_lengths,
    new_counts,
    extend_flags,
):
    ways = lax.axis_size("tensor")
    places = lax.axis_size("seq")
    mine = lax.axis_index("tensor")
    rows, features = tokens.shape
    cached = cache_keys.shape[0]
    heads = bias_table.shape[1]
    width = cache_keys.shape[1]
    trainer_rows = joined_weight.shape[0]
    hidden_units = upward_weight.shape[1] // ways
    attn_width = output_weight.shape[1]
    columns = attn_width + 2 * hidden_units
    span = bucket_index.shape[0] + 1

    weights = (joined_weight, output_weight, upward_weight, downward_weight)
    *joined_blocks, forward = pl.pallas_call(
        cut_kernel,
        name="cut",
        out_shape=[jax.ShapeDtypeStruct((trainer_rows, 3 * width), HALF)] * ways
        + [jax.ShapeDtypeStruct((ways, trainer_rows, columns), HALF)],
        in_specs=[HBM] * 4,
        out_specs=[VMEM] * (1 + ways),
        scratch_shapes=[pltpu.VMEM(weight.shape, FULL) for weight in weights]
        + [pltpu.SemaphoreType.DMA((4,))],
        compiler_params=params(CUT_GRANT),
    )(*weights)
    own_joined, joined_blocks = joined_blocks[0], exchange(joined_blocks)

    normed, bias = pl.pallas_call(
        prepare_kernel,
        name="prepare",
        out_shape=[
            jax.ShapeDtypeStruct((rows, features), HALF),
            jax.ShapeDtypeStruct((heads, rows, cached + rows), FULL),
        ],
        in_specs=[ANY, HBM, HBM, HBM, VMEM, VMEM, VMEM, VMEM],
        out_specs=[VMEM, VMEM],
        scratch_shapes=[
            pltpu.SMEM((3,) + new_counts.shape, jnp.int32),
            pltpu.VMEM((1, span), jnp.int32),
            pltpu.SemaphoreType.DMA((3,)),
        ],
        compiler_params=params(VMEM_GRANT),
        cost_estimate=cost(2 * 10**10, 4 * 10**6),
    )(
        own_joined,
        cached_lengths,
        extend_flags,
        new_counts,
        tokens,
        first_gain.reshape(1, features),
        bias_table.T,
        bucket_index.reshape(1, span - 1),
    )

    if places == 8:
        lead = (places, ways, trainer_rows)
        joined = stack(joined_blocks)
        near, far, normed = together(*first_hops(joined), normed)
        held = whole_hop(joined, near, far)
        joined_pieces, joined_all = with_cores(held)
    else:
        lead = (features,)
        natural = [lax.select_n(mine ^ t, *joined_blocks) for t in range(ways)]
        joined_pieces, joined_all = [None], [natural_gather(jnp.stack(natural))]
    forward = owners_blocks(forward)

    attention = pl.pallas_call(
        functools.partial(attend_kernel, joined_pieces),
        name="attend",
        out_shape=jax.ShapeDtypeStruct((rows, width), HALF),
        in_specs=[VMEM, VMEM, VMEM, VMEM] + [ANY] * len(joined_all),
        out_specs=VMEM,
        scratch_shapes=[pltpu.VMEM(lead + (3 * width,), HALF), pltpu.SemaphoreType.DMA((8,))],
        compiler_params=params(VMEM_GRANT),
        cost_estimate=cost(ATTEND_COST, 6 * 10**6),
    )(normed, cache_keys, cache_values, bias, *joined_all)

    attended = [attention] + [swap(attention, "tensor", k) for k in range(1, ways)]
    if places == 8:
        forward_pieces, forward_all = with_cores(half_hops(forward, *first_hops(forward)))
    else:
        forward_pieces, forward_all = [None], [natural_gather(forward)]
    share = rows // ways
    own, *sends = pl.pallas_call(
        functools.partial(layer_kernel, forward_pieces, ways),
        name="layer",
        out_shape=[jax.ShapeDtypeStruct((share, features), FULL)]
        + [jax.ShapeDtypeStruct((share, features), HALF)] * (ways - 1),
        in_specs=[VMEM, VMEM] + [VMEM] * ways + [ANY] * len(forward_all),
        out_specs=[VMEM] * ways,
        scratch_shapes=[
            pltpu.VMEM(lead + (attn_width,), HALF),
            pltpu.VMEM(lead + (hidden_units,), HALF),
            pltpu.VMEM(lead + (hidden_units,), HALF),
            pltpu.VMEM((rows, attn_width), HALF),
            pltpu.VMEM((rows, features), FULL),
            pltpu.VMEM((rows, features), FULL),
            pltpu.SemaphoreType.DMA((3, len(forward_all))),
        ],
        compiler_params=params(VMEM_GRANT),
        cost_estimate=cost(2 * 10**9, 8 * 10**6),
    )(tokens, second_gain.reshape(1, features), *attended, *forward_all)

    shared = [swap(send, "tensor", k) for k, send in enumerate(sends, 1) if k > 1]
    neighbour, shared[0] = together(sends[0], shared[0])
    total = own
    for block in [swap(neighbour, "tensor", 1)] + shared:
        total = total + block.astype(FULL)
    return total.astype(HALF)


def solution(mesh):
    return jax.shard_map(
        shards,
        mesh=mesh,
        in_specs=(
            P("seq", None),
            P("seq", "tensor"),
            P("seq", "tensor"),
            P(("seq", "tensor"), None),
            P(("seq", "tensor"), None),
            P(("seq", "tensor"), None),
            P(("seq", "tensor"), None),
            P(),
            P(),
            P(None, "tensor"),
            P(),
            P(),
            P(),
            P(),
        ),
        out_specs=P(("seq", "tensor"), None),
        check_vma=False,
    )
```
